256 devices in a mesh: section: 8 (over x_lo, y), ctx: 32 (over z, x_hi, core).
Axes of the slice: x: 4 (x_hi: 2, x_lo: 2; x = x_hi * 2 + x_lo), y: 4, z: 8, core: 2. Of those that a mesh axis runs over, the one named last changes fastest.
Arguments:
- embeds: bfloat16 [4096, 2048], P('ctx'), may hold values from -7 to 7
- q_weight: bfloat16 [8, 2048, 1024], P('section'), may hold values from -1 to 1
- out_weight: bfloat16 [8, 1024, 2048], P('section'), may hold values from -0.1875 to 0.1875
- norm_gain: bfloat16 [8, 2048], P('section'), may hold values from 0.3984375 to 2.5
- kv_weight: bfloat16 [2048, 512], replicated, may hold values from -1 to 1
- kv_gain: bfloat16 [2048], replicated, may hold values from 0.5 to 1.5
- block_slot: int32 [32], replicated, may hold values from 0 to 31, each once
Outputs:
- layer_out: bfloat16 [8, 4096, 2048], P('section', 'ctx')
- decode_cache: bfloat16 [32, 128, 512], P('ctx', None, 'section')
The draws below stay inside these ranges and needn't reach their ends.
Inputs may be any that keep to these rules, and one draw needn't show every extreme that they name: `block_slot`: every slot is named by exactly one block; slot s is kept by ctx index s // 1.
All inputs are finite; a program needn't handle non-finite values.
Results may differ from the reference program's by a relative error of at most 0.025.
Values may be sent and summed in bfloat16 or wider, within the bound.
A program may use at most 128 MiB of HBM per device.

```python
import math
import jax
import jax.numpy as jnp
from jax import lax

MODEL_WIDTH = 2048
QUERY_HEADS = 16
KEY_VALUE_HEADS = 4
HEAD_SIZE = 64
BLOCK = 128
ITERS = 3
LAYERS = 8
TOKEN_COUNT = 4096
NBLOCKS = 32
KEY_VALUE_WIDTH = 512


def draw_embeds(key, part):
    key = jax.random.fold_in(key, 11)
    value_rows = jnp.clip(jax.random.normal(key, (TOKEN_COUNT, MODEL_WIDTH), jnp.float32), -6.0, 6.0)
    return value_rows.astype(jnp.bfloat16)


def draw_q_weight(key, part):
    key = jax.random.fold_in(key, 12)
    base = jnp.clip(jax.random.normal(key, (LAYERS, MODEL_WIDTH, QUERY_HEADS * HEAD_SIZE), jnp.float32), -6.0, 6.0) * MODEL_WIDTH ** (-0.5)
    return jnp.clip(base, -1.0, 1.0).astype(jnp.bfloat16)


def draw_kv_weight(key, part):
    key = jax.random.fold_in(key, 13)
    base = jnp.clip(jax.random.normal(key, (MODEL_WIDTH, KEY_VALUE_WIDTH), jnp.float32), -6.0, 6.0) * MODEL_WIDTH ** (-0.5)
    return jnp.clip(base, -1.0, 1.0).astype(jnp.bfloat16)


def level_of(key, extent, pieces, low, top_value):
    loudness, own = 1.0, jax.random.fold_in(key, 6)
    for position, blocks in pieces:
        steps = jnp.exp(jax.random.uniform(jax.random.fold_in(own, position), (blocks,), jnp.float32, low / len(pieces), top_value / len(pieces)))
        loudness = loudness * jnp.repeat(steps, extent[position] // blocks).reshape([-1 if axis == position else 1 for axis in range(len(extent))])
    return loudness


def scatter_about(rng, extent, spread, bound, cuts=(), kind=jnp.bfloat16):
    level = level_of(rng, extent, cuts, -0.22, 0.18) if cuts else 1.0
    result = jax.random.normal(rng, extent, jnp.float32) * spread * level
    return jnp.minimum(jnp.maximum(result, -bound), bound).astype(kind)


def setup_inputs(seed: int = 0) -> dict:
    arg_keys = jax.random.split(jax.random.key(seed), 8)
    embeds = draw_embeds(jax.random.fold_in(arg_keys[7], 71), 0)
    q_weight = draw_q_weight(jax.random.fold_in(arg_keys[7], 71), 0)
    out_weight = scatter_about(arg_keys[2], (LAYERS, QUERY_HEADS * HEAD_SIZE, MODEL_WIDTH), (QUERY_HEADS * HEAD_SIZE) ** -0.5, 0.1875, ((0, 8),))
    norm_gain = jnp.clip(jnp.exp(math.log(2.5) - 1.8364954 * jax.random.uniform(arg_keys[3], (LAYERS, MODEL_WIDTH), jnp.float32) ** level_of(arg_keys[3], (LAYERS, MODEL_WIDTH), ((0, 8),), -0.2, 0.2)), 0.3984375, 2.5).astype(jnp.bfloat16)
    kv_weight = draw_kv_weight(jax.random.fold_in(arg_keys[7], 71), 0)
    kv_gain = jnp.clip(1.0 + 0.1 * jax.random.normal(arg_keys[5], (MODEL_WIDTH,), jnp.float32), 0.5, 1.5).astype(jnp.bfloat16)
    block_slot = jax.random.permutation(arg_keys[6], NBLOCKS).astype(jnp.int32)
    return {"embeds": embeds, "q_weight": q_weight, "out_weight": out_weight, "norm_gain": norm_gain, "kv_weight": kv_weight, "kv_gain": kv_gain, "block_slot": block_slot}


EPS = 1e-05
HIGHEST = lax.Precision.HIGHEST

def normalize(value_rows, gain):
    wide = value_rows.astype(jnp.float32)
    factor = lax.rsqrt(lax.optimization_barrier(jnp.mean(wide * wide, axis=-1, keepdims=True)) + EPS)
    return wide * factor * gain.astype(jnp.float32)

def project_cache(hidden, kv_gain, kv_weight):
    normed = normalize(hidden, kv_gain).astype(jnp.bfloat16)
    return jnp.dot(normed, kv_weight, preferred_element_type=jnp.float32).astype(jnp.bfloat16)

def online_update(loop_state, query_rows, qpos, key_rows, value_rows, kpos):
    maxima, totals, accum = loop_state
    scores = jnp.einsum('igrd,jgd->grij', query_rows.astype(jnp.float32), key_rows.astype(jnp.float32), precision=HIGHEST) * HEAD_SIZE ** (-0.5)
    allowed = kpos[None, :] <= qpos[:, None]
    scores = jnp.where(allowed, scores, -1e+30)
    newmax = jnp.maximum(maxima, lax.optimization_barrier(jnp.max(scores, axis=-1)))
    probs = jnp.where(allowed, jnp.exp(scores - newmax[..., None]), 0.0)
    decay = jnp.exp(maxima - newmax)
    rounded = lax.optimization_barrier(probs.astype(jnp.bfloat16)).astype(jnp.float32)
    update = jnp.einsum('grij,jgd->grid', rounded, value_rows.astype(jnp.float32), precision=HIGHEST)
    return (newmax, decay * totals + lax.optimization_barrier(jnp.sum(probs, axis=-1)), decay[..., None] * accum + update)

def attend(query_rows, top_cache):
    block_length = math.gcd(TOKEN_COUNT, 512)
    count = TOKEN_COUNT // block_length
    half_width = KEY_VALUE_HEADS * HEAD_SIZE
    query_groups = QUERY_HEADS // KEY_VALUE_HEADS
    key_rows = top_cache[:, :half_width].reshape(TOKEN_COUNT, KEY_VALUE_HEADS, HEAD_SIZE)
    value_rows = top_cache[:, half_width:].reshape(TOKEN_COUNT, KEY_VALUE_HEADS, HEAD_SIZE)

    def per_block(index):
        qstart = index * block_length
        qrows = lax.dynamic_slice_in_dim(query_rows, qstart, block_length, 0)
        qpos = qstart + jnp.arange(block_length, dtype=jnp.int32)
        initial_state = (jnp.full((KEY_VALUE_HEADS, query_groups, block_length), -1e+30, jnp.float32), jnp.zeros((KEY_VALUE_HEADS, query_groups, block_length), jnp.float32), jnp.zeros((KEY_VALUE_HEADS, query_groups, block_length, HEAD_SIZE), jnp.float32))

        def jacobi_sweep(loop_state, key_index):
            key_offset = key_index * block_length

            def update(inner):
                kpos = key_offset + jnp.arange(block_length, dtype=jnp.int32)
                return online_update(inner, qrows, qpos, lax.dynamic_slice_in_dim(key_rows, key_offset, block_length, 0), lax.dynamic_slice_in_dim(value_rows, key_offset, block_length, 0), kpos)
            return (lax.cond(key_offset > qstart + block_length - 1, lambda inner: inner, update, loop_state), None)
        state, _ = lax.scan(jacobi_sweep, initial_state, jnp.arange(count, dtype=jnp.int32))
        merged = state[2] / state[1][..., None]
        return merged.transpose(2, 0, 1, 3).reshape(block_length, QUERY_HEADS * HEAD_SIZE)
    return lax.map(per_block, jnp.arange(count, dtype=jnp.int32)).reshape(TOKEN_COUNT, QUERY_HEADS * HEAD_SIZE)

def layer(hidden, gain, q_matrix, o_matrix, top_cache):
    normed = normalize(hidden, gain).astype(jnp.bfloat16)
    query_rows = jnp.dot(normed, q_matrix, preferred_element_type=jnp.float32).astype(jnp.bfloat16)
    query_rows = query_rows.reshape(TOKEN_COUNT, KEY_VALUE_HEADS, QUERY_HEADS // KEY_VALUE_HEADS, HEAD_SIZE)
    mixed = attend(query_rows, top_cache).astype(jnp.bfloat16)
    return (hidden.astype(jnp.float32) + jnp.dot(mixed, o_matrix, preferred_element_type=jnp.float32)).astype(jnp.bfloat16)

def reference(embeds, q_weight, out_weight, norm_gain, kv_weight, kv_gain, block_slot):
    top_cache = project_cache(embeds, kv_gain, kv_weight)
    inputs = [embeds for _ in range(LAYERS)]
    outputs = inputs
    for step in range(ITERS):
        outputs = [layer(inputs[index], norm_gain[index], q_weight[index], out_weight[index], top_cache) for index in range(LAYERS)]
        inputs = [embeds] + outputs[:-1]
        top_cache = project_cache(outputs[-1], kv_gain, kv_weight)
    blocks = top_cache.reshape(NBLOCKS, BLOCK, KEY_VALUE_WIDTH)
    decode_cache = jnp.zeros_like(blocks).at[block_slot].set(blocks)
    return (jnp.stack(outputs), decode_cache)
```

```python
import jax
import jax.numpy as jnp
from jax import lax
from jax.experimental import pallas as pl
from jax.experimental.pallas import tpu as pltpu
from jax.sharding import PartitionSpec as P

BF16, F32 = jnp.bfloat16, jnp.float32
MESH = pl.DeviceIdType.MESH
WIDTH = 2048
ROWS = 128
HEADS = 16
KV_HEADS = 4
HEAD = 64
ITERS = 3
EPS = 1e-05
NEG = -1e30
QSCALE = HEAD**-0.5 * 1.4426950408889634


def normalize(rows, gain):
    wide = rows.astype(F32)
    factor = lax.rsqrt(jnp.mean(wide * wide, axis=-1, keepdims=True) + EPS)
    return (wide * factor * gain.astype(F32)).astype(BF16)


def kernel(
    embeds, q_weight, out_weight, kv_weight, norm_gain, kv_gain, block_slot,
    layer_out, decode,
    wq, wo, wkv, hid, xs, kv, qst, qbuf, mst, mbuf, hout, ka, kb, vt, mx, acc,
    fx, grid, pick, land, inv,
    load_sem, kvd_s, kvd_r, sib_s, sib_r, q_s, q_r, m_s, m_r, h_s, h_r, ks_s, ks_r,
    f1_s, f1_r, f2_s, f2_r, f3_s, f3_r,
):
    s, c = lax.axis_index("section"), lax.axis_index("ctx")
    x_lo, y = s // 4, s % 4
    z, xh, core = c // 4, (c // 2) % 2, c % 2
    xc = c % 4
    top = s == 7
    sib = z * 4 + xh * 2 + (1 - core)

    loads = [
        pltpu.make_async_copy(src, dst, load_sem.at[i])
        for i, (src, dst) in enumerate(
            ((embeds, hid[0]), (kv_weight, wkv), (q_weight.at[0], wq), (out_weight.at[0], wo))
        )
    ]
    for copy in loads:
        copy.start()

    barrier = pltpu.get_barrier_semaphore()

    def greet(section, ctx):
        pl.semaphore_signal(barrier, inc=1, device_id=(section, ctx), device_id_type=MESH)

    for d in range(1, 8):
        greet((s + d) % 8, c)
    for dz in range(8):
        for dx in range(2):
            if dz or dx:
                greet(s, ((z + dz) % 8) * 4 + ((xh + dx) % 2) * 2 + core)
    greet(s, sib)
    greet(s, z * 4 + (1 - xh) * 2 + (1 - core))
    pl.semaphore_wait(barrier, 7 + 15 + 2)

    def send(src, dst, ssem, rsem, section, ctx):
        return pltpu.make_async_remote_copy(
            src_ref=src, dst_ref=dst, send_sem=ssem, recv_sem=rsem,
            device_id=(section, ctx), device_id_type=MESH,
        )

    def kv_out(t, z2, x2):
        return send(kv[t].at[c], kv[t].at[c], kvd_s.at[t, z2 * 2 + x2],
                    kvd_r.at[t, z * 2 + xh], s, z2 * 4 + x2 * 2 + core)

    def kv_in(t, z2, x2):
        b = z2 * 4 + x2 * 2 + core
        return send(kv[t].at[b], kv[t].at[b], kvd_s.at[t, z2 * 2 + x2],
                    kvd_r.at[t, z2 * 2 + x2], s, sib)

    def sib_out(t, z2, x2):
        b = z2 * 4 + x2 * 2 + core
        return send(kv[t].at[b], kv[t].at[b], sib_s.at[t, z2 * 2 + x2],
                    sib_r.at[t, z2 * 2 + x2], s, sib)

    def sib_in(t, z2, x2):
        b = z2 * 4 + x2 * 2 + 1 - core
        return send(kv[t].at[b], kv[t].at[b], sib_s.at[t, z2 * 2 + x2],
                    sib_r.at[t, z2 * 2 + x2], s, sib)

    def q_out(t, j):
        return send(qst[t].at[j], qbuf[t].at[y], q_s.at[t, j], q_r.at[t, y], x_lo * 4 + j, c)

    def q_in(t, j):
        return send(qst[t].at[j], qbuf[t].at[j], q_s.at[t, j], q_r.at[t, j], x_lo * 4 + j, c)

    def m_out(t, i):
        return send(mst[t].at[i], mbuf[t].at[y], m_s.at[t, i], m_r.at[t, y], x_lo * 4 + i, c)

    def m_in(t, j):
        return send(mst[t].at[j], mbuf[t].at[j], m_s.at[t, j], m_r.at[t, j], x_lo * 4 + j, c)

    def h_out(t):
        return send(hout[t], hid[t + 1], h_s.at[t], h_r.at[t], (s + 1) % 8, c)

    def ks_out(t, s2):
        dst = kv[t].at[c] if t < ITERS else fx
        return send(xs[t].at[s2 % 4], dst, ks_s.at[t - 1, s2], ks_r.at[t - 1], s2, c)

    def f1_out(i):
        return send(fx.at[pl.ds(16 * i, 16)], grid.at[xc, z], f1_s.at[i], f1_r.at[z], s, i * 4 + xc)

    def f1_in(i):
        return send(fx.at[pl.ds(0, 16)], grid.at[xc, i], f1_s.at[i], f1_r.at[i], s, i * 4 + xc)

    def f2_out(d):
        other = (xc + d) % 4
        return send(grid.at[xc], grid.at[xc], f2_s.at[d], f2_r.at[d], s, z * 4 + other)

    def f2_in(d):
        other = (xc + 4 - d) % 4
        return send(grid.at[other], grid.at[other], f2_s.at[d], f2_r.at[d], s, z * 4 + other)

    def f3_out(i):
        return send(pick.at[i], land.at[z], f3_s.at[i], f3_r.at[z], s, i * 4 + xc)

    def f3_in(i):
        return send(pick.at[i], land.at[i], f3_s.at[i], f3_r.at[i], s, i * 4 + xc)

    lane = lax.broadcasted_iota(jnp.int32, (ROWS, 128), 1)

    def project(hidden, t):
        normed = normalize(hidden, kv_gain[...])
        rows = jnp.dot(normed, wkv[...], preferred_element_type=F32)
        for j in range(KV_HEADS):
            a, half = 128 * (j // 2), j % 2
            keys, values = rows[:, a:a + 128], rows[:, 256 + a:384 + a]
            if half == 0:
                both = jnp.where(lane < HEAD, keys, pltpu.roll(values, HEAD, 1))
            else:
                both = jnp.where(lane < HEAD, pltpu.roll(keys, HEAD, 1), values)
            xs[t][j] = both.astype(BF16)

    def spread(t):
        sib_out(t, z, xh).start()
        kv_out(t, z, 1 - xh).start()
        for d in range(1, 8):
            @pl.when(z + d < 8)
            def _():
                for x2 in range(2):
                    kv_out(t, z + d, x2).start()

    def spread_done(t):
        sib_out(t, z, xh).wait_send()
        kv_out(t, z, 1 - xh).wait_send()
        for d in range(1, 8):
            @pl.when(z + d < 8)
            def _():
                for x2 in range(2):
                    kv_out(t, z + d, x2).wait_send()

    def relay_early(t):
        for z2 in range(7):
            @pl.when(z2 < z)
            def _():
                for x2 in range(2):
                    kv_in(t, z2, x2).wait_recv()
                    sib_out(t, z2, x2).start()

    def relay_own(t):
        kv_in(t, z, 1 - xh).wait_recv()
        sib_out(t, z, 1 - xh).start()

    def relay_done(t):
        sib_out(t, z, 1 - xh).wait_send()
        for z2 in range(7):
            @pl.when(z2 < z)
            def _():
                for x2 in range(2):
                    sib_out(t, z2, x2).wait_send()

    def queries(t):
        normed = normalize(hid[t][...], norm_gain[...])
        for j in range(KV_HEADS):
            rows = jnp.dot(normed, wq[:, 256 * j:256 * j + 256], preferred_element_type=F32)
            rows = (rows * QSCALE).astype(BF16)

            @pl.when(y == j)
            def _():
                for p in range(2):
                    qbuf[t][j, p] = rows[:, 128 * p:128 * p + 128]

            @pl.when(y != j)
            def _():
                for p in range(2):
                    qst[t][j, p] = rows[:, 128 * p:128 * p + 128]
                q_out(t, j).start()

    key_row = lax.broadcasted_iota(jnp.int32, (128, 512), 0)
    key_lane = lax.broadcasted_iota(jnp.int32, (512, 128), 1)

    def prepare(t, z2):
        x = kv[t][pl.ds(z2 * 4, 4)].reshape(512, 128).astype(F32)
        r = pltpu.roll(x, HEAD, 1)
        at = pl.ds(pl.multiple_of(z2 * 512, 512), 512)
        ka[at, :] = jnp.where(key_lane < HEAD, x, 0.0).astype(BF16)
        kb[at, :] = jnp.where(key_lane < HEAD, 0.0, r).astype(BF16)
        vt[:, at] = jnp.where(key_row < HEAD, r.T, 1.0).astype(BF16)

    def unit(t, z2, masked):
        at = pl.ds(pl.multiple_of(z2 * 512, 512), 512)
        qq = qbuf[t][...].reshape(1024, 128)
        for h, keys in enumerate((ka, kb)):
            scores = lax.dot_general(
                keys[at, :], qq, (((1,), (1,)), ((), ())), preferred_element_type=F32
            )
            if masked:
                kpos = lax.broadcasted_iota(jnp.int32, (512, 1024), 0)
                qpos = lax.broadcasted_iota(jnp.int32, (512, 1024), 1) % ROWS + xc * ROWS
                scores = jnp.where(kpos <= qpos, scores, NEG)
            old = mx[h]
            new = jnp.maximum(old, jnp.max(scores, axis=0, keepdims=True))
            decay = jnp.exp2(old - new)
            mx[h] = new
            probs = jnp.exp2(scores - new).astype(BF16)
            acc[h] = acc[h] * decay + jnp.dot(vt[0:72, at], probs, preferred_element_type=F32)

    def attend(t):
        mx[...] = jnp.full(mx.shape, NEG, F32)
        acc[...] = jnp.zeros(acc.shape, F32)
        for z2 in range(7):
            @pl.when(z2 < z)
            def _():
                for x2 in range(2):
                    sib_in(t, z2, x2).wait_recv()
                prepare(t, z2)

        def body(z2, carry):
            unit(t, z2, False)
            return carry

        lax.fori_loop(0, z, body, 0)
        sib_in(t, z, 0).wait_recv()
        sib_in(t, z, 1).wait_recv()
        prepare(t, z)
        unit(t, z, True)
        for i in range(4):
            for p in range(2):
                at = slice((2 * i + p) * 128, (2 * i + p) * 128 + 128)
                halves = [acc[h, 0:HEAD, at] / acc[h, HEAD:HEAD + 1, at] for h in range(2)]
                rows = jnp.concatenate(halves, axis=0).T.astype(BF16)

                @pl.when(y == i)
                def _():
                    mbuf[t][i, :, 128 * p:128 * p + 128] = rows

                @pl.when(y != i)
                def _():
                    mst[t][i, :, 128 * p:128 * p + 128] = rows

            @pl.when(y != i)
            def _():
                m_out(t, i).start()

    def finish(t, out):
        for j in range(4):
            @pl.when(y != j)
            def _():
                m_in(t, j).wait_recv()
        mixed = jnp.concatenate([mbuf[t][j] for j in range(4)], axis=1)
        for n in range(4):
            at = slice(512 * n, 512 * n + 512)
            grown = jnp.dot(mixed, wo[:, at], preferred_element_type=F32)
            out[:, at] = (hid[t][:, at].astype(F32) + grown).astype(BF16)

    loads[0].wait()
    loads[1].wait()
    project(hid[0][...], 0)
    kv[0][c] = xs[0][y]
    spread(0)
    loads[2].wait()
    queries(0)

    @pl.when(s == 0)
    def _():
        for t in range(1, ITERS):
            hid[t][...] = hid[0][...]

    def invert(b, found):
        slot = block_slot[b]
        return tuple(jnp.where(slot == i * 4 + xc, b, f) for i, f in enumerate(found))

    found = lax.fori_loop(0, 32, invert, (jnp.int32(0),) * 8)
    for i in range(8):
        inv[i] = found[i]

    relay_own(0)
    relay_early(0)
    for t in range(ITERS):
        for j in range(4):
            @pl.when(y != j)
            def _():
                q_in(t, j).wait_recv()
        attend(t)
        if t == 0:
            loads[3].wait()
        last = t + 1 == ITERS
        finish(t, layer_out.at[0] if last else hout[t])
        if not last:
            @pl.when(s < 7)
            def _():
                h_out(t).start()

        @pl.when(top)
        def _():
            project(layer_out[0] if last else hout[t][...], t + 1)
            for s2 in range(7):
                ks_out(t + 1, s2).start()
            if last:
                fx[...] = xs[t + 1][3]
            else:
                kv[t + 1][c] = xs[t + 1][3]

        @pl.when(s < 7)
        def _():
            ks_out(t + 1, 0).wait_recv()

        if not last:
            spread(t + 1)
            relay_early(t + 1)

            @pl.when(s > 0)
            def _():
                h_out(t).wait_recv()

            queries(t + 1)
            relay_own(t + 1)

    for i in range(8):
        @pl.when(z != i)
        def _():
            f1_out(i).start()
    grid[xc, z] = fx[pl.ds(pl.multiple_of(z * 16, 16), 16), :]
    for i in range(8):
        @pl.when(z != i)
        def _():
            f1_in(i).wait_recv()
    for d in range(1, 4):
        f2_out(d).start()
    for d in range(1, 4):
        f2_in(d).wait_recv()
    for i in range(8):
        b = inv[i]
        rows = grid[b % 4, b // 4]

        @pl.when(z != i)
        def _():
            pick[i] = rows
            f3_out(i).start()

        @pl.when(z == i)
        def _():
            land[i] = rows
    for i in range(8):
        @pl.when(z != i)
        def _():
            f3_in(i).wait_recv()
    rows = land[...].reshape(ROWS, 128)

    @pl.when(x_lo == 0)
    def _():
        decode[0] = rows[:, :HEAD]

    @pl.when(x_lo != 0)
    def _():
        decode[0] = rows[:, HEAD:]

    for t in range(ITERS):
        spread_done(t)
        relay_done(t)
        for j in range(4):
            @pl.when(y != j)
            def _():
                q_out(t, j).wait_send()
                m_out(t, j).wait_send()
        if t + 1 < ITERS:
            @pl.when(s < 7)
            def _():
                h_out(t).wait_send()

        @pl.when(top)
        def _():
            for s2 in range(7):
                ks_out(t + 1, s2).wait_send()
    for i in range(8):
        @pl.when(z != i)
        def _():
            f1_out(i).wait_send()
            f3_out(i).wait_send()
    for d in range(1, 4):
        f2_out(d).wait_send()


def body(embeds, q_weight, out_weight, norm_gain, kv_weight, kv_gain, block_slot):
    vmem = pl.BlockSpec(memory_space=pltpu.VMEM)
    hbm = pl.BlockSpec(memory_space=pl.ANY)
    dma = pltpu.SemaphoreType.DMA
    return pl.pallas_call(
        kernel,
        out_shape=(
            jax.ShapeDtypeStruct((1, ROWS, WIDTH), BF16),
            jax.ShapeDtypeStruct((1, ROWS, HEAD), BF16),
        ),
        in_specs=[hbm, hbm, hbm, hbm, vmem, vmem, pl.BlockSpec(memory_space=pltpu.SMEM)],
        out_specs=(vmem, vmem),
        scratch_shapes=[
            pltpu.VMEM((WIDTH, 1024), BF16),
            pltpu.VMEM((1024, WIDTH), BF16),
            pltpu.VMEM((WIDTH, 512), BF16),
            ITERS * (pltpu.VMEM((ROWS, WIDTH), BF16),),
            (ITERS + 1) * (pltpu.VMEM((4, ROWS, 128), BF16),),
            ITERS * (pltpu.VMEM((32, ROWS, 128), BF16),),
            ITERS * (pltpu.VMEM((4, 2, ROWS, 128), BF16),),
            ITERS * (pltpu.VMEM((4, 2, ROWS, 128), BF16),),
            ITERS * (pltpu.VMEM((4, ROWS, 256), BF16),),
            ITERS * (pltpu.VMEM((4, ROWS, 256), BF16),),
            (ITERS - 1) * (pltpu.VMEM((ROWS, WIDTH), BF16),),
            pltpu.VMEM((4096, 128), BF16),
            pltpu.VMEM((4096, 128), BF16),
            pltpu.VMEM((128, 4096), BF16),
            pltpu.VMEM((2, 1, 1024), F32),
            pltpu.VMEM((2, 72, 1024), F32),
            pltpu.VMEM((ROWS, 128), BF16),
            pltpu.VMEM((4, 8, 16, 128), BF16),
            pltpu.VMEM((8, 16, 128), BF16),
            pltpu.VMEM((8, 16, 128), BF16),
            pltpu.SMEM((8,), jnp.int32),
            dma((4,)),
            dma((ITERS, 16)), dma((ITERS, 16)), dma((ITERS, 16)), dma((ITERS, 16)),
            dma((ITERS, 4)), dma((ITERS, 4)), dma((ITERS, 4)), dma((ITERS, 4)),
            dma((ITERS,)), dma((ITERS,)), dma((ITERS, 8)), dma((ITERS,)),
            dma((8,)), dma((8,)), dma((4,)), dma((4,)), dma((8,)), dma((8,)),
        ],
        compiler_params=pltpu.CompilerParams(
            collective_id=0, has_side_effects=True, vmem_limit_bytes=56 << 20
        ),
        cost_estimate=pl.CostEstimate(
            flops=20 * 10**9, bytes_accessed=12 * 2**20, transcendentals=10**7
        ),
    )(embeds, q_weight, out_weight, kv_weight, norm_gain, kv_gain.reshape(1, WIDTH), block_slot)


def solution(mesh):
    return jax.shard_map(
        body,
        mesh=mesh,
        in_specs=(
            P("ctx", None),
            P("section", None, None),
            P("section", None, None),
            P("section", None),
            P(),
            P(),
            P(),
        ),
        out_specs=(P("section", "ctx", None), P("ctx", None, "section")),
        check_vma=False,
    )
```

```python
import jax
import jax.numpy as jnp
from jax import lax
from jax.experimental import pallas as pl
from jax.experimental.pallas import tpu as pltpu
from jax.sharding import PartitionSpec as P

BF16, F32 = jnp.bfloat16, jnp.float32
MESH = pl.DeviceIdType.MESH
WIDTH = 2048
ROWS = 128
HEADS = 16
KV_HEADS = 4
HEAD = 64
ITERS = 3
EPS = 1e-05
NEG = -1e30
QSCALE = HEAD**-0.5 * 1.4426950408889634


def normalize(rows, gain):
    wide = rows.astype(F32)
    factor = lax.rsqrt(jnp.mean(wide * wide, axis=-1, keepdims=True) + EPS)
    return (wide * factor * gain.astype(F32)).astype(BF16)


def kernel(
    embeds, q_weight, out_weight, kv_weight, norm_gain, kv_gain, block_slot,
    layer_out, decode,
    wq, wo, wkv, hid, xs, xf, kv, qst, qbuf, mst, mbuf, hout, ka, kb, vt, mx, acc, qacc, fin,
    load_sem, kvd_s, kvd_r, sib_s, sib_r, q_s, q_r, m_s, m_r, h_s, h_r, ks_s, ks_r,
    fin_s, fin_r,
):
    s, c = lax.axis_index("section"), lax.axis_index("ctx")
    x_lo, y = s // 4, s % 4
    z, xh, core = c // 4, (c // 2) % 2, c % 2
    xc = c % 4
    top = s == 7
    sib = z * 4 + xh * 2 + (1 - core)

    rows0 = hid[0]
    loads = [
        pltpu.make_async_copy(src, dst, load_sem.at[i])
        for i, (src, dst) in enumerate(
            ((embeds, rows0), (kv_weight, wkv), (q_weight.at[0], wq), (out_weight.at[0], wo))
        )
    ]
    for copy in loads:
        copy.start()

    barrier = pltpu.get_barrier_semaphore()

    def greet(section, ctx):
        pl.semaphore_signal(barrier, inc=1, device_id=(section, ctx), device_id_type=MESH)

    for d in range(1, 8):
        greet((s + d) % 8, c)
    for d in range(1, 32):
        greet(s, (c + d) % 32)
    pl.semaphore_wait(barrier, 7 + 31)

    def send(src, dst, ssem, rsem, section, ctx):
        return pltpu.make_async_remote_copy(
            src_ref=src, dst_ref=dst, send_sem=ssem, recv_sem=rsem,
            device_id=(section, ctx), device_id_type=MESH,
        )

    def kv_out(t, d, x2):
        return send(kv[t][0].at[xc], kv[t][d].at[xc], kvd_s.at[t, d * 2 + x2],
                    kvd_r.at[t, d * 2 + xh], s, (z + d) * 4 + x2 * 2 + core)

    def kv_in(t, d, x2):
        b = x2 * 2 + core
        return send(kv[t][d].at[b], kv[t][d].at[b], kvd_s.at[t, d * 2 + x2],
                    kvd_r.at[t, d * 2 + x2], s, sib)

    def sib_out(t, d, x2):
        b = x2 * 2 + core
        return send(kv[t][d].at[b], kv[t][d].at[b], sib_s.at[t, d * 2 + x2],
                    sib_r.at[t, d * 2 + x2], s, sib)

    def sib_in(t, d, x2):
        b = x2 * 2 + 1 - core
        return send(kv[t][d].at[b], kv[t][d].at[b], sib_s.at[t, d * 2 + x2],
                    sib_r.at[t, d * 2 + x2], s, sib)

    def q_out(t, j):
        return send(qst[t].at[j], qbuf[t].at[y], q_s.at[t, j], q_r.at[t, y], x_lo * 4 + j, c)

    def q_in(t, j):
        return send(qst[t].at[j], qbuf[t].at[j], q_s.at[t, j], q_r.at[t, j], x_lo * 4 + j, c)

    def m_out(t, i):
        return send(mst[t].at[i], mbuf[t].at[y], m_s.at[t, i], m_r.at[t, y], x_lo * 4 + i, c)

    def m_in(t, j):
        return send(mst[t].at[j], mbuf[t].at[j], m_s.at[t, j], m_r.at[t, j], x_lo * 4 + j, c)

    def h_out(t, n):
        return send(hout[t][n], hid[t + 1][n], h_s.at[t, n], h_r.at[t, n], (s + 1) % 8, c)

    def ks_out(t, s2):
        if t < ITERS:
            return send(xs[t].at[s2 % 4], kv[t][0].at[xc], ks_s.at[t - 1, s2], ks_r.at[t - 1], s2, c)
        return send(xf.at[s2], fin.at[c], ks_s.at[t - 1, s2], ks_r.at[t - 1], s2, c)

    def fin_out(d):
        return send(fin.at[c], fin.at[c], fin_s.at[d], fin_r.at[d], s, (c + d) % 32)

    def fin_in(d):
        b = (c + 32 - d) % 32
        return send(fin.at[b], fin.at[b], fin_s.at[d], fin_r.at[d], s, b)

    lane = lax.broadcasted_iota(jnp.int32, (ROWS, 128), 1)

    def cache_rows(hidden):
        normed = normalize(hidden, kv_gain[...].reshape(1, WIDTH))
        return jnp.dot(normed, wkv[...], preferred_element_type=F32)

    def project(hidden, t):
        rows = cache_rows(hidden)
        for j in range(KV_HEADS):
            a, half = 128 * (j // 2), j % 2
            keys, values = rows[:, a:a + 128], rows[:, 256 + a:384 + a]
            if half == 0:
                both = jnp.where(lane < HEAD, keys, pltpu.roll(values, HEAD, 1))
            else:
                both = jnp.where(lane < HEAD, pltpu.roll(keys, HEAD, 1), values)
            xs[t][j] = both.astype(BF16)

    def project_last(hidden):
        rows = cache_rows(hidden)
        low = lane[:HEAD] < HEAD
        for s2 in range(8):
            a = 128 * (s2 // 2)
            upper, lower = rows[:HEAD, a:a + 128], rows[HEAD:, a:a + 128]
            if s2 % 2 == 0:
                both = jnp.where(low, upper, pltpu.roll(lower, HEAD, 1))
            else:
                both = jnp.where(low, pltpu.roll(upper, HEAD, 1), lower)
            xf[s2] = both.astype(BF16)

    def spread(t):
        sib_out(t, 0, xh).start()
        kv_out(t, 0, 1 - xh).start()
        for d in range(1, 8):
            @pl.when(z + d < 8)
            def _():
                for x2 in range(2):
                    kv_out(t, d, x2).start()

    def spread_done(t):
        sib_out(t, 0, xh).wait_send()
        kv_out(t, 0, 1 - xh).wait_send()
        for d in range(1, 8):
            @pl.when(z + d < 8)
            def _():
                for x2 in range(2):
                    kv_out(t, d, x2).wait_send()

    def relay(t, d):
        for x2 in range(2):
            kv_in(t, d, x2).wait_recv()
            sib_out(t, d, x2).start()

    def relay_own(t):
        kv_in(t, 0, 1 - xh).wait_recv()
        sib_out(t, 0, 1 - xh).start()

    def relay_done(t):
        sib_out(t, 0, 1 - xh).wait_send()
        for d in range(1, 8):
            @pl.when(d <= z)
            def _():
                for x2 in range(2):
                    sib_out(t, d, x2).wait_send()

    def place_queries(t, j, rows):
        @pl.when(y == j)
        def _():
            for p in range(2):
                qbuf[t][j, p] = rows[:, 128 * p:128 * p + 128]

        @pl.when(y != j)
        def _():
            for p in range(2):
                qst[t][j, p] = rows[:, 128 * p:128 * p + 128]
            q_out(t, j).start()

    def first_queries():
        normed = normalize(rows0[...], norm_gain[...])
        for j in range(KV_HEADS):
            rows = jnp.dot(normed, wq[:, 256 * j:256 * j + 256], preferred_element_type=F32)
            place_queries(0, j, (rows * QSCALE).astype(BF16))

    def queries(t):
        squares = jnp.zeros((ROWS, 1), F32)
        for n in range(4):
            @pl.when(s > 0)
            def _():
                h_out(t - 1, n).wait_recv()

            at = slice(512 * n, 512 * n + 512)
            wide = hid[t][n][...].astype(F32)
            squares += jnp.sum(wide * wide, axis=-1, keepdims=True)
            gained = (wide * norm_gain[:, at].astype(F32)).astype(BF16)
            for j in range(KV_HEADS):
                cols = slice(256 * j, 256 * j + 256)
                part = jnp.dot(gained, wq[at, cols], preferred_element_type=F32)
                if n == 0:
                    qacc[:, cols] = part
                elif n < 3:
                    qacc[:, cols] += part
                else:
                    factor = lax.rsqrt(squares / WIDTH + EPS) * QSCALE
                    place_queries(t, j, ((qacc[:, cols] + part) * factor).astype(BF16))

    key_row = lax.broadcasted_iota(jnp.int32, (128, 512), 0)
    key_lane = lax.broadcasted_iota(jnp.int32, (512, 128), 1)

    def prepare(t, d):
        for x2 in range(2):
            sib_in(t, d, x2).wait_recv()
        x = kv[t][d][...].reshape(512, 128).astype(F32)
        r = pltpu.roll(x, HEAD, 1)
        at = slice(512 * d, 512 * d + 512)
        ka[at, :] = jnp.where(key_lane < HEAD, x, 0.0).astype(BF16)
        kb[at, :] = jnp.where(key_lane < HEAD, 0.0, r).astype(BF16)
        vt[:, at] = jnp.where(key_row < HEAD, r.T, 1.0).astype(BF16)

    def unit(t, d, masked):
        at = pl.ds(pl.multiple_of(d * 512, 512), 512)
        qq = qbuf[t][...].reshape(1024, 128)
        for h, keys in enumerate((ka, kb)):
            scores = lax.dot_general(
                keys[at, :], qq, (((1,), (1,)), ((), ())), preferred_element_type=F32
            )
            if masked:
                kpos = lax.broadcasted_iota(jnp.int32, (512, 1024), 0)
                qpos = lax.broadcasted_iota(jnp.int32, (512, 1024), 1) % ROWS + xc * ROWS
                scores = jnp.where(kpos <= qpos, scores, NEG)
            scores = scores.reshape(64, 8, 1024)
            top8 = jnp.max(scores, axis=0)
            for k in (4, 2, 1):
                top8 = jnp.maximum(top8, pltpu.roll(top8, k, 0))
            old = mx[h]
            new = jnp.maximum(old, top8)
            decay = jnp.exp2(old - new)
            mx[h] = new
            probs = jnp.exp2(scores - new[None]).astype(BF16).reshape(512, 1024)
            grown = jnp.dot(vt[0:72, at], probs, preferred_element_type=F32)
            acc[h] = (acc[h].reshape(9, 8, 1024) * decay[None]).reshape(72, 1024) + grown

    def wait_queries(t):
        for j in range(4):
            @pl.when(y != j)
            def _():
                q_in(t, j).wait_recv()

    def start_state():
        mx[...] = jnp.full(mx.shape, NEG, F32)
        acc[...] = jnp.zeros(acc.shape, F32)

    def first_units():
        start_state()
        relay_own(0)
        prepare(0, 0)

        @pl.when(z > 0)
        def _():
            relay(0, 1)

        wait_queries(0)
        unit(0, 0, True)

        def step(d, carry):
            for near in range(1, 8):
                @pl.when(d == near)
                def _():
                    if near < 7:
                        @pl.when(near < z)
                        def _():
                            relay(0, near + 1)

                    prepare(0, near)

            unit(0, d, False)
            return carry

        lax.fori_loop(1, z + 1, step, 0)

    def units(t):
        start_state()
        for d in range(7, 0, -1):
            @pl.when(d <= z)
            def _():
                prepare(t, d)

        wait_queries(t)

        def step(d, carry):
            unit(t, d, False)
            return carry

        lax.fori_loop(1, z + 1, step, 0)
        prepare(t, 0)
        unit(t, 0, True)

    def send_mixed(t):
        for i in range(4):
            for p in range(2):
                at = slice((2 * i + p) * 128, (2 * i + p) * 128 + 128)
                halves = [acc[h, 0:HEAD, at] / acc[h, HEAD:HEAD + 1, at] for h in range(2)]
                rows = jnp.concatenate(halves, axis=0).T.astype(BF16)

                @pl.when(y == i)
                def _():
                    mbuf[t][i, :, 128 * p:128 * p + 128] = rows

                @pl.when(y != i)
                def _():
                    mst[t][i, :, 128 * p:128 * p + 128] = rows

            @pl.when(y != i)
            def _():
                m_out(t, i).start()

    def finish(t):
        for j in range(4):
            @pl.when(y != j)
            def _():
                m_in(t, j).wait_recv()
        mixed = jnp.concatenate([mbuf[t][j] for j in range(4)], axis=1)
        for n in range(4):
            at = slice(512 * n, 512 * n + 512)
            grown = jnp.dot(mixed, wo[:, at], preferred_element_type=F32)
            before = rows0[:, at] if t == 0 else hid[t][n][...]
            out = (before.astype(F32) + grown).astype(BF16)
            if t + 1 == ITERS:
                layer_out[0, :, at] = out
            else:
                hout[t][n][...] = out

                @pl.when(s < 7)
                def _():
                    h_out(t, n).start()

    loads[0].wait()
    loads[1].wait()
    project(rows0[...], 0)
    kv[0][0][xc] = xs[0][y]
    spread(0)
    loads[2].wait()
    first_queries()

    @pl.when(s == 0)
    def _():
        for t in range(1, ITERS):
            for n in range(4):
                hid[t][n][...] = rows0[:, 512 * n:512 * n + 512]

    for t in range(ITERS):
        if t == 0:
            first_units()
        else:
            units(t)
        send_mixed(t)
        if t == 0:
            loads[3].wait()
        finish(t)
        if t + 1 < ITERS:
            @pl.when(top)
            def _():
                project(jnp.concatenate([hout[t][n][...] for n in range(4)], axis=1), t + 1)
                for s2 in range(7):
                    ks_out(t + 1, s2).start()
                kv[t + 1][0][xc] = xs[t + 1][3]

            @pl.when(s < 7)
            def _():
                ks_out(t + 1, 0).wait_recv()

            spread(t + 1)
            for d in range(7, 0, -1):
                @pl.when(d <= z)
                def _():
                    relay(t + 1, d)

            queries(t + 1)
            relay_own(t + 1)

    @pl.when(top)
    def _():
        project_last(layer_out[0])
        for s2 in range(7):
            ks_out(ITERS, s2).start()
        fin[c] = xf[7]

    @pl.when(s < 7)
    def _():
        ks_out(ITERS, 0).wait_recv()

    for d in range(1, 32):
        fin_out(d).start()

    def find(b, found):
        return jnp.where(block_slot[b] == c, b, found)

    block = lax.fori_loop(0, 32, find, jnp.int32(0))
    for d in range(1, 32):
        fin_in(d).wait_recv()
    rows = fin[block]
    decode[0, 0:HEAD, :] = rows[:, :HEAD]
    decode[0, HEAD:, :] = rows[:, HEAD:]

    for t in range(ITERS):
        spread_done(t)
        relay_done(t)
        for j in range(4):
            @pl.when(y != j)
            def _():
                q_out(t, j).wait_send()
                m_out(t, j).wait_send()
        if t + 1 < ITERS:
            @pl.when(s < 7)
            def _():
                for n in range(4):
                    h_out(t, n).wait_send()

        @pl.when(top)
        def _():
            for s2 in range(7):
                ks_out(t + 1, s2).wait_send()
    for d in range(1, 32):
        fin_out(d).wait_send()


def body(embeds, q_weight, out_weight, norm_gain, kv_weight, kv_gain, block_slot):
    vmem = pl.BlockSpec(memory_space=pltpu.VMEM)
    hbm = pl.BlockSpec(memory_space=pl.ANY)
    dma = pltpu.SemaphoreType.DMA
    return pl.pallas_call(
        kernel,
        out_shape=(
            jax.ShapeDtypeStruct((1, ROWS, WIDTH), BF16),
            jax.ShapeDtypeStruct((1, ROWS, HEAD), BF16),
        ),
        in_specs=[hbm, hbm, hbm, hbm, vmem, vmem, pl.BlockSpec(memory_space=pltpu.SMEM)],
        out_specs=(vmem, vmem),
        scratch_shapes=[
            pltpu.VMEM((WIDTH, 1024), BF16),
            pltpu.VMEM((1024, WIDTH), BF16),
            pltpu.VMEM((WIDTH, 512), BF16),
            (pltpu.VMEM((ROWS, WIDTH), BF16),) + (ITERS - 1) * (4 * (pltpu.VMEM((ROWS, 512), BF16),),),
            ITERS * (pltpu.VMEM((4, ROWS, 128), BF16),),
            pltpu.VMEM((8, HEAD, 128), BF16),
            ITERS * (8 * (pltpu.VMEM((4, ROWS, 128), BF16),),),
            ITERS * (pltpu.VMEM((4, 2, ROWS, 128), BF16),),
            ITERS * (pltpu.VMEM((4, 2, ROWS, 128), BF16),),
            ITERS * (pltpu.VMEM((4, ROWS, 256), BF16),),
            ITERS * (pltpu.VMEM((4, ROWS, 256), BF16),),
            (ITERS - 1) * (4 * (pltpu.VMEM((ROWS, 512), BF16),),),
            pltpu.VMEM((4096, 128), BF16),
            pltpu.VMEM((4096, 128), BF16),
            pltpu.VMEM((128, 4096), BF16),
            pltpu.VMEM((2, 8, 1024), F32),
            pltpu.VMEM((2, 72, 1024), F32),
            pltpu.VMEM((ROWS, 1024), F32),
            pltpu.VMEM((32, HEAD, 128), BF16),
            dma((4,)),
            dma((ITERS, 16)), dma((ITERS, 16)), dma((ITERS, 16)), dma((ITERS, 16)),
            dma((ITERS, 4)), dma((ITERS, 4)), dma((ITERS, 4)), dma((ITERS, 4)),
            dma((ITERS, 4)), dma((ITERS, 4)), dma((ITERS, 8)), dma((ITERS,)),
            dma((32,)), dma((32,)),
        ],
        compiler_params=pltpu.CompilerParams(
            collective_id=0, has_side_effects=True, vmem_limit_bytes=56 << 20
        ),
        cost_estimate=pl.CostEstimate(
            flops=20 * 10**9, bytes_accessed=12 * 2**20, transcendentals=10**7
        ),
    )(embeds, q_weight, out_weight, kv_weight, norm_gain, kv_gain, block_slot)


def solution(mesh):
    return jax.shard_map(
        body,
        mesh=mesh,
        in_specs=(
            P("ctx", None),
            P("section", None, None),
            P("section", None, None),
            P("section", None),
            P(),
            P(),
            P(),
        ),
        out_specs=(P("section", "ctx", None), P("ctx", None, "section")),
        check_vma=False,
    )
```

```python
import jax
import jax.numpy as jnp
from jax import lax
from jax.experimental import pallas as pl
from jax.experimental.pallas import tpu as pltpu
from jax.sharding import PartitionSpec as P

BF16, F32 = jnp.bfloat16, jnp.float32
MESH = pl.DeviceIdType.MESH
WIDTH = 2048
ROWS = 128
HEADS = 16
KV_HEADS = 4
HEAD = 64
ITERS = 3
EPS = 1e-05
NEG = -1e30
QSCALE = HEAD**-0.5 * 1.4426950408889634


def normalize(rows, gain):
    wide = rows.astype(F32)
    factor = lax.rsqrt(jnp.mean(wide * wide, axis=-1, keepdims=True) + EPS)
    return (wide * factor * gain.astype(F32)).astype(BF16)


def kernel(
    embeds, q_weight, out_weight, kv_weight, norm_gain, kv_gain, block_slot,
    layer_out, decode,
    wq, wo, wkv, hid, xs, xf, kv, qst, qbuf, mst, mbuf, hout, ka, kb, vt, mx, acc, qacc, fin, pick, land,
    load_sem, kvd_s, kvd_r, sib_s, sib_r, q_s, q_r, m_s, m_r, h_s, h_r, ks_s, ks_r,
    fin_s, fin_r, pick_s, pick_r,
):
    s, c = lax.axis_index("section"), lax.axis_index("ctx")
    x_lo, y = s // 4, s % 4
    z, xh, core = c // 4, (c // 2) % 2, c % 2
    xc = c % 4
    top = s == 7
    me = x_lo * 2 + y % 2
    sib = z * 4 + xh * 2 + (1 - core)

    rows0 = hid[0]
    loads = [
        pltpu.make_async_copy(src, dst, load_sem.at[i])
        for i, (src, dst) in enumerate(
            ((embeds, rows0), (kv_weight, wkv), (q_weight.at[0], wq), (out_weight.at[0], wo))
        )
    ]
    for copy in loads:
        copy.start()

    barrier = pltpu.get_barrier_semaphore()

    def greet(section, ctx):
        pl.semaphore_signal(barrier, inc=1, device_id=(section, ctx), device_id_type=MESH)

    for d in range(1, 8):
        greet((s + d) % 8, c)
    for d in range(1, 8):
        for x2 in range(2):
            greet(s, ((z + d) % 8) * 4 + x2 * 2 + core)
    for d in range(1, 4):
        greet(s, z * 4 + (xc + d) % 4)
    pl.semaphore_wait(barrier, 7 + 14 + 3)

    def send(src, dst, ssem, rsem, section, ctx):
        return pltpu.make_async_remote_copy(
            src_ref=src, dst_ref=dst, send_sem=ssem, recv_sem=rsem,
            device_id=(section, ctx), device_id_type=MESH,
        )

    def kv_out(t, d, x2):
        return send(kv[t][0].at[xc], kv[t][d].at[xc], kvd_s.at[t, d * 2 + x2],
                    kvd_r.at[t, d * 2 + xh], s, (z + d) * 4 + x2 * 2 + core)

    def kv_in(t, d, x2):
        b = x2 * 2 + core
        return send(kv[t][d].at[b], kv[t][d].at[b], kvd_s.at[t, d * 2 + x2],
                    kvd_r.at[t, d * 2 + x2], s, sib)

    def sib_out(t, d, x2):
        b = x2 * 2 + core
        return send(kv[t][d].at[b], kv[t][d].at[b], sib_s.at[t, d * 2 + x2],
                    sib_r.at[t, d * 2 + x2], s, sib)

    def sib_in(t, d, x2):
        b = x2 * 2 + 1 - core
        return send(kv[t][d].at[b], kv[t][d].at[b], sib_s.at[t, d * 2 + x2],
                    sib_r.at[t, d * 2 + x2], s, sib)

    def member(m):
        return (m // 2) * 4 + (y // 2) * 2 + m % 2

    def q_out(t, j):
        return send(qst[t].at[j], qbuf[t].at[me], q_s.at[t, j], q_r.at[t, me], member(j), c)

    def q_in(t, j):
        return send(qst[t].at[j], qbuf[t].at[j], q_s.at[t, j], q_r.at[t, j], member(j), c)

    def m_out(t, i):
        return send(mst[t].at[i], mbuf[t].at[me], m_s.at[t, i], m_r.at[t, me], member(i), c)

    def m_in(t, j):
        return send(mst[t].at[j], mbuf[t].at[j], m_s.at[t, j], m_r.at[t, j], member(j), c)

    def h_out(t, n):
        return send(hout[t][n], hid[t + 1][n], h_s.at[t, n], h_r.at[t, n], (s + 1) % 8, c)

    def ks_out(t, s2):
        if t < ITERS:
            return send(xs[t].at[(s2 // 4) * 2 + s2 % 2], kv[t][0].at[xc], ks_s.at[t - 1, s2], ks_r.at[t - 1], s2, c)
        return send(xf.at[s2], fin.at[z], ks_s.at[t - 1, s2], ks_r.at[t - 1], s2, c)

    def fin_out(d):
        return send(fin.at[z], fin.at[z], fin_s.at[d], fin_r.at[d], s, ((z + d) % 8) * 4 + xc)

    def fin_in(d):
        b = (z + 8 - d) % 8
        return send(fin.at[b], fin.at[b], fin_s.at[d], fin_r.at[d], s, b * 4 + xc)

    def pick_out(d):
        other = (xc + d) % 4
        return send(pick.at[d], land.at[d], pick_s.at[d], pick_r.at[d], s, z * 4 + other)

    lane = lax.broadcasted_iota(jnp.int32, (ROWS, 128), 1)

    def cache_rows(hidden):
        normed = normalize(hidden, kv_gain[...].reshape(1, WIDTH))
        return jnp.dot(normed, wkv[...], preferred_element_type=F32)

    def project(hidden, t):
        rows = cache_rows(hidden)
        for j in range(KV_HEADS):
            a, half = 128 * (j // 2), j % 2
            keys, values = rows[:, a:a + 128], rows[:, 256 + a:384 + a]
            if half == 0:
                both = jnp.where(lane < HEAD, keys, pltpu.roll(values, HEAD, 1))
            else:
                both = jnp.where(lane < HEAD, pltpu.roll(keys, HEAD, 1), values)
            xs[t][j] = both.astype(BF16)

    def project_last(hidden):
        rows = cache_rows(hidden)
        low = lane[:HEAD] < HEAD
        for s2 in range(8):
            a = 128 * (s2 // 2)
            upper, lower = rows[:HEAD, a:a + 128], rows[HEAD:, a:a + 128]
            if s2 % 2 == 0:
                both = jnp.where(low, upper, pltpu.roll(lower, HEAD, 1))
            else:
                both = jnp.where(low, pltpu.roll(upper, HEAD, 1), lower)
            xf[s2] = both.astype(BF16)

    def spread(t):
        sib_out(t, 0, xh).start()
        kv_out(t, 0, 1 - xh).start()
        for d in range(1, 8):
            @pl.when(z + d < 8)
            def _():
                for x2 in range(2):
                    kv_out(t, d, x2).start()

    def spread_done(t):
        sib_out(t, 0, xh).wait_send()
        kv_out(t, 0, 1 - xh).wait_send()
        for d in range(1, 8):
            @pl.when(z + d < 8)
            def _():
                for x2 in range(2):
                    kv_out(t, d, x2).wait_send()

    def relay(t, d):
        for x2 in range(2):
            kv_in(t, d, x2).wait_recv()
            sib_out(t, d, x2).start()

    def relay_own(t):
        kv_in(t, 0, 1 - xh).wait_recv()
        sib_out(t, 0, 1 - xh).start()

    def relay_done(t):
        sib_out(t, 0, 1 - xh).wait_send()
        for d in range(1, 8):
            @pl.when(d <= z)
            def _():
                for x2 in range(2):
                    sib_out(t, d, x2).wait_send()

    def place_queries(t, j, rows):
        @pl.when(me == j)
        def _():
            for p in range(2):
                qbuf[t][j, p] = rows[:, 128 * p:128 * p + 128]

        @pl.when(me != j)
        def _():
            for p in range(2):
                qst[t][j, p] = rows[:, 128 * p:128 * p + 128]
            q_out(t, j).start()

    def first_queries():
        normed = normalize(rows0[...], norm_gain[...])
        for j in range(KV_HEADS):
            rows = jnp.dot(normed, wq[:, 256 * j:256 * j + 256], preferred_element_type=F32)
            place_queries(0, j, (rows * QSCALE).astype(BF16))

    def queries(t):
        squares = jnp.zeros((ROWS, 1), F32)
        for n in range(4):
            @pl.when(s > 0)
            def _():
                h_out(t - 1, n).wait_recv()

            at = slice(512 * n, 512 * n + 512)
            wide = hid[t][n][...].astype(F32)
            squares += jnp.sum(wide * wide, axis=-1, keepdims=True)
            gained = (wide * norm_gain[:, at].astype(F32)).astype(BF16)
            for j in range(KV_HEADS):
                cols = slice(256 * j, 256 * j + 256)
                part = jnp.dot(gained, wq[at, cols], preferred_element_type=F32)
                if n == 0:
                    qacc[:, cols] = part
                elif n < 3:
                    qacc[:, cols] += part
                else:
                    factor = lax.rsqrt(squares / WIDTH + EPS) * QSCALE
                    place_queries(t, j, ((qacc[:, cols] + part) * factor).astype(BF16))

    key_row = lax.broadcasted_iota(jnp.int32, (128, 512), 0)
    key_lane = lax.broadcasted_iota(jnp.int32, (512, 128), 1)

    def prepare(t, d):
        for x2 in range(2):
            sib_in(t, d, x2).wait_recv()
        x = kv[t][d][...].reshape(512, 128).astype(F32)
        r = pltpu.roll(x, HEAD, 1)
        at = slice(512 * d, 512 * d + 512)
        ka[at, :] = jnp.where(key_lane < HEAD, x, 0.0).astype(BF16)
        kb[at, :] = jnp.where(key_lane < HEAD, 0.0, r).astype(BF16)
        vt[:, at] = jnp.where(key_row < HEAD, r.T, 1.0).astype(BF16)

    def unit(t, d, masked):
        at = pl.ds(pl.multiple_of(d * 512, 512), 512)
        qq = qbuf[t][...].reshape(1024, 128)
        for h, keys in enumerate((ka, kb)):
            scores = lax.dot_general(
                keys[at, :], qq, (((1,), (1,)), ((), ())), preferred_element_type=F32
            )
            if masked:
                kpos = lax.broadcasted_iota(jnp.int32, (512, 1024), 0)
                qpos = lax.broadcasted_iota(jnp.int32, (512, 1024), 1) % ROWS + xc * ROWS
                scores = jnp.where(kpos <= qpos, scores, NEG)
            scores = scores.reshape(64, 8, 1024)
            top8 = jnp.max(scores, axis=0)
            for k in (4, 2, 1):
                top8 = jnp.maximum(top8, pltpu.roll(top8, k, 0))
            old = mx[h]
            new = jnp.maximum(old, top8)
            decay = jnp.exp2(old - new)
            mx[h] = new
            probs = jnp.exp2(scores - new[None]).astype(BF16).reshape(512, 1024)
            grown = jnp.dot(vt[0:72, at], probs, preferred_element_type=F32)
            acc[h] = (acc[h].reshape(9, 8, 1024) * decay[None]).reshape(72, 1024) + grown

    def wait_queries(t):
        for j in range(4):
            @pl.when(me != j)
            def _():
                q_in(t, j).wait_recv()

    def start_state():
        mx[...] = jnp.full(mx.shape, NEG, F32)
        acc[...] = jnp.zeros(acc.shape, F32)

    def first_units():
        start_state()
        relay_own(0)
        prepare(0, 0)

        @pl.when(z > 0)
        def _():
            relay(0, 1)

        wait_queries(0)
        unit(0, 0, True)

        def step(d, carry):
            for near in range(1, 8):
                @pl.when(d == near)
                def _():
                    if near < 7:
                        @pl.when(near < z)
                        def _():
                            relay(0, near + 1)

                    prepare(0, near)

            unit(0, d, False)
            return carry

        lax.fori_loop(1, z + 1, step, 0)

    def units(t):
        start_state()
        for d in range(1, 8):
            @pl.when(d == z)
            def _():
                relay(t, d)

        wait_queries(t)

        def step(i, carry):
            d = z - i
            for near in range(1, 8):
                @pl.when(d == near)
                def _():
                    if near > 1:
                        relay(t, near - 1)
                    prepare(t, near)

            unit(t, d, False)
            return carry

        lax.fori_loop(0, z, step, 0)
        relay_own(t)
        prepare(t, 0)
        unit(t, 0, True)

    def send_mixed(t):
        for i in range(4):
            for p in range(2):
                at = slice((2 * i + p) * 128, (2 * i + p) * 128 + 128)
                halves = [acc[h, 0:HEAD, at] / acc[h, HEAD:HEAD + 1, at] for h in range(2)]
                rows = jnp.concatenate(halves, axis=0).T.astype(BF16)

                @pl.when(me == i)
                def _():
                    mbuf[t][i, :, 128 * p:128 * p + 128] = rows

                @pl.when(me != i)
                def _():
                    mst[t][i, :, 128 * p:128 * p + 128] = rows

            @pl.when(me != i)
            def _():
                m_out(t, i).start()

    def finish(t):
        for j in range(4):
            @pl.when(me != j)
            def _():
                m_in(t, j).wait_recv()
        mixed = jnp.concatenate([mbuf[t][j] for j in range(4)], axis=1)
        for n in range(4):
            at = slice(512 * n, 512 * n + 512)
            grown = jnp.dot(mixed, wo[:, at], preferred_element_type=F32)
            before = rows0[:, at] if t == 0 else hid[t][n][...]
            out = (before.astype(F32) + grown).astype(BF16)
            if t + 1 == ITERS:
                layer_out[0, :, at] = out
            else:
                hout[t][n][...] = out

                @pl.when(s < 7)
                def _():
                    h_out(t, n).start()

    loads[0].wait()
    loads[1].wait()
    project(rows0[...], 0)
    kv[0][0][xc] = xs[0][me]
    spread(0)
    loads[2].wait()
    first_queries()

    @pl.when(s == 0)
    def _():
        for t in range(1, ITERS):
            for n in range(4):
                hid[t][n][...] = rows0[:, 512 * n:512 * n + 512]

    for t in range(ITERS):
        if t == 0:
            first_units()
        else:
            units(t)
        send_mixed(t)
        if t == 0:
            loads[3].wait()
        finish(t)
        if t + 1 < ITERS:
            @pl.when(top)
            def _():
                project(jnp.concatenate([hout[t][n][...] for n in range(4)], axis=1), t + 1)
                for s2 in range(7):
                    ks_out(t + 1, s2).start()
                kv[t + 1][0][xc] = xs[t + 1][3]

            queries(t + 1)

            @pl.when(s < 7)
            def _():
                ks_out(t + 1, 0).wait_recv()

            spread(t + 1)

    @pl.when(top)
    def _():
        project_last(layer_out[0])
        for s2 in range(7):
            ks_out(ITERS, s2).start()
        fin[z] = xf[7]

    @pl.when(s < 7)
    def _():
        ks_out(ITERS, 0).wait_recv()

    for d in range(1, 8):
        fin_out(d).start()

    def find(b, found):
        slot = block_slot[b]
        return tuple(jnp.where(slot == z * 4 + (xc + d) % 4, b, f) for d, f in enumerate(found))

    found = lax.fori_loop(0, 32, find, (jnp.int32(0),) * 4)
    for d in range(1, 8):
        fin_in(d).wait_recv()
    for d in range(1, 4):
        pick[d] = fin[found[d] // 4]
        pick_out(d).start()
    rows = fin[found[0] // 4]
    for d in range(1, 4):
        pick_out(d).wait_recv()
        rows = jnp.where(found[0] % 4 == (xc + 4 - d) % 4, land[d], rows)
    decode[0, 0:HEAD, :] = rows[:, :HEAD]
    decode[0, HEAD:, :] = rows[:, HEAD:]

    for t in range(ITERS):
        spread_done(t)
        relay_done(t)
        for j in range(4):
            @pl.when(me != j)
            def _():
                q_out(t, j).wait_send()
                m_out(t, j).wait_send()
        if t + 1 < ITERS:
            @pl.when(s < 7)
            def _():
                for n in range(4):
                    h_out(t, n).wait_send()

        @pl.when(top)
        def _():
            for s2 in range(7):
                ks_out(t + 1, s2).wait_send()
    for d in range(1, 8):
        fin_out(d).wait_send()
    for d in range(1, 4):
        pick_out(d).wait_send()


def body(embeds, q_weight, out_weight, norm_gain, kv_weight, kv_gain, block_slot):
    vmem = pl.BlockSpec(memory_space=pltpu.VMEM)
    hbm = pl.BlockSpec(memory_space=pl.ANY)
    dma = pltpu.SemaphoreType.DMA
    return pl.pallas_call(
        kernel,
        out_shape=(
            jax.ShapeDtypeStruct((1, ROWS, WIDTH), BF16),
            jax.ShapeDtypeStruct((1, ROWS, HEAD), BF16),
        ),
        in_specs=[hbm, hbm, hbm, hbm, vmem, vmem, pl.BlockSpec(memory_space=pltpu.SMEM)],
        out_specs=(vmem, vmem),
        scratch_shapes=[
            pltpu.VMEM((WIDTH, 1024), BF16),
            pltpu.VMEM((1024, WIDTH), BF16),
            pltpu.VMEM((WIDTH, 512), BF16),
            (pltpu.VMEM((ROWS, WIDTH), BF16),) + (ITERS - 1) * (4 * (pltpu.VMEM((ROWS, 512), BF16),),),
            ITERS * (pltpu.VMEM((4, ROWS, 128), BF16),),
            pltpu.VMEM((8, HEAD, 128), BF16),
            ITERS * (8 * (pltpu.VMEM((4, ROWS, 128), BF16),),),
            ITERS * (pltpu.VMEM((4, 2, ROWS, 128), BF16),),
            ITERS * (pltpu.VMEM((4, 2, ROWS, 128), BF16),),
            ITERS * (pltpu.VMEM((4, ROWS, 256), BF16),),
            ITERS * (pltpu.VMEM((4, ROWS, 256), BF16),),
            (ITERS - 1) * (4 * (pltpu.VMEM((ROWS, 512), BF16),),),
            pltpu.VMEM((4096, 128), BF16),
            pltpu.VMEM((4096, 128), BF16),
            pltpu.VMEM((128, 4096), BF16),
            pltpu.VMEM((2, 8, 1024), F32),
            pltpu.VMEM((2, 72, 1024), F32),
            pltpu.VMEM((ROWS, 1024), F32),
            pltpu.VMEM((8, HEAD, 128), BF16),
            pltpu.VMEM((4, HEAD, 128), BF16),
            pltpu.VMEM((4, HEAD, 128), BF16),
            dma((4,)),
            dma((ITERS, 16)), dma((ITERS, 16)), dma((ITERS, 16)), dma((ITERS, 16)),
            dma((ITERS, 4)), dma((ITERS, 4)), dma((ITERS, 4)), dma((ITERS, 4)),
            dma((ITERS, 4)), dma((ITERS, 4)), dma((ITERS, 8)), dma((ITERS,)),
            dma((8,)), dma((8,)), dma((4,)), dma((4,)),
        ],
        compiler_params=pltpu.CompilerParams(
            collective_id=0, has_side_effects=True, vmem_limit_bytes=56 << 20
        ),
        cost_estimate=pl.CostEstimate(
            flops=20 * 10**9, bytes_accessed=12 * 2**20, transcendentals=10**7
        ),
    )(embeds, q_weight, out_weight, kv_weight, norm_gain, kv_gain, block_slot)


def solution(mesh):
    return jax.shard_map(
        body,
        mesh=mesh,
        in_specs=(
            P("ctx", None),
            P("section", None, None),
            P("section", None, None),
            P("section", None),
            P(),
            P(),
            P(),
        ),
        out_specs=(P("section", "ctx", None), P("ctx", None, "section")),
        check_vma=False,
    )
```

```python
import jax
import jax.numpy as jnp
from jax import lax
from jax.experimental import pallas as pl
from jax.experimental.pallas import tpu as pltpu
from jax.sharding import PartitionSpec as P

BF16, F32 = jnp.bfloat16, jnp.float32
MESH = pl.DeviceIdType.MESH
WIDTH = 2048
ROWS = 128
HEADS = 16
KV_HEADS = 4
HEAD = 64
ITERS = 3
EPS = 1e-05
NEG = -1e30
QSCALE = HEAD**-0.5 * 1.4426950408889634


def normalize(rows, gain):
    wide = rows.astype(F32)
    factor = lax.rsqrt(jnp.mean(wide * wide, axis=-1, keepdims=True) + EPS)
    return (wide * factor * gain.astype(F32)).astype(BF16)


def kernel(
    embeds, q_weight, out_weight, kv_weight, norm_gain, kv_gain, block_slot,
    layer_out, decode,
    wq, wo, wkv, hid, xs, xf, kv, qst, qbuf, mst, mbuf, hout, ka, kb, vt, mx, acc, sc, qacc, fin,
    load_sem, kvd_s, kvd_r, sib_s, sib_r, q_s, q_r, m_s, m_r, h_s, h_r, ks_s, ks_r,
    fin_s, fin_r,
):
    s, c = lax.axis_index("section"), lax.axis_index("ctx")
    x_lo, y = s // 4, s % 4
    z, xh, core = c // 4, (c // 2) % 2, c % 2
    xc = c % 4
    top = s == 7
    me = x_lo * 2 + y % 2
    sib = z * 4 + xh * 2 + (1 - core)

    rows0 = hid[0]
    loads = [
        pltpu.make_async_copy(src, dst, load_sem.at[i])
        for i, (src, dst) in enumerate(
            ((embeds, rows0), (kv_weight, wkv), (q_weight.at[0], wq), (out_weight.at[0], wo))
        )
    ]
    for copy in loads:
        copy.start()

    barrier = pltpu.get_barrier_semaphore()

    def greet(section, ctx):
        pl.semaphore_signal(barrier, inc=1, device_id=(section, ctx), device_id_type=MESH)

    for d in range(1, 8):
        greet((s + d) % 8, c)
    for d in range(1, 32):
        greet(s, (c + d) % 32)
    pl.semaphore_wait(barrier, 7 + 31)

    def send(src, dst, ssem, rsem, section, ctx):
        return pltpu.make_async_remote_copy(
            src_ref=src, dst_ref=dst, send_sem=ssem, recv_sem=rsem,
            device_id=(section, ctx), device_id_type=MESH,
        )

    def kv_out(t, d, x2):
        return send(kv[t][0].at[xc], kv[t][d].at[xc], kvd_s.at[t, d * 2 + x2],
                    kvd_r.at[t, d * 2 + xh], s, (z + d) * 4 + x2 * 2 + core)

    def kv_in(t, d, x2):
        b = x2 * 2 + core
        return send(kv[t][d].at[b], kv[t][d].at[b], kvd_s.at[t, d * 2 + x2],
                    kvd_r.at[t, d * 2 + x2], s, sib)

    def sib_out(t, d, x2):
        b = x2 * 2 + core
        return send(kv[t][d].at[b], kv[t][d].at[b], sib_s.at[t, d * 2 + x2],
                    sib_r.at[t, d * 2 + x2], s, sib)

    def sib_in(t, d, x2):
        b = x2 * 2 + 1 - core
        return send(kv[t][d].at[b], kv[t][d].at[b], sib_s.at[t, d * 2 + x2],
                    sib_r.at[t, d * 2 + x2], s, sib)

    def member(m):
        return (m // 2) * 4 + (y // 2) * 2 + m % 2

    def q_out(t, j):
        return send(qst[t].at[j], qbuf[t].at[me], q_s.at[t, j], q_r.at[t, me], member(j), c)

    def q_in(t, j):
        return send(qst[t].at[j], qbuf[t].at[j], q_s.at[t, j], q_r.at[t, j], member(j), c)

    def m_out(t, i):
        return send(mst[t].at[i], mbuf[t].at[me], m_s.at[t, i], m_r.at[t, me], member(i), c)

    def m_in(t, j):
        return send(mst[t].at[j], mbuf[t].at[j], m_s.at[t, j], m_r.at[t, j], member(j), c)

    def h_out(t, n):
        return send(hout[t][n], hid[t + 1][n], h_s.at[t, n], h_r.at[t, n], (s + 1) % 8, c)

    def ks_out(t, s2):
        if t < ITERS:
            return send(xs[t].at[(s2 // 4) * 2 + s2 % 2], kv[t][0].at[xc], ks_s.at[t - 1, s2], ks_r.at[t - 1], s2, c)
        return send(xf.at[s2], fin.at[c], ks_s.at[t - 1, s2], ks_r.at[t - 1], s2, c)

    def fin_out(d):
        return send(fin.at[c], fin.at[c], fin_s.at[d], fin_r.at[d], s, (c + d) % 32)

    def fin_in(d):
        b = (c + 32 - d) % 32
        return send(fin.at[b], fin.at[b], fin_s.at[d], fin_r.at[d], s, b)

    lane = lax.broadcasted_iota(jnp.int32, (ROWS, 128), 1)

    def cache_rows(hidden):
        normed = normalize(hidden, kv_gain[...].reshape(1, WIDTH))
        return jnp.dot(normed, wkv[...], preferred_element_type=F32)

    def project(hidden, t):
        rows = cache_rows(hidden)
        for j in range(KV_HEADS):
            a, half = 128 * (j // 2), j % 2
            keys, values = rows[:, a:a + 128], rows[:, 256 + a:384 + a]
            if half == 0:
                both = jnp.where(lane < HEAD, keys, pltpu.roll(values, HEAD, 1))
            else:
                both = jnp.where(lane < HEAD, pltpu.roll(keys, HEAD, 1), values)
            xs[t][j] = both.astype(BF16)

    def project_last(hidden):
        rows = cache_rows(hidden)
        low = lane[:HEAD] < HEAD
        for s2 in range(8):
            a = 128 * (s2 // 2)
            upper, lower = rows[:HEAD, a:a + 128], rows[HEAD:, a:a + 128]
            if s2 % 2 == 0:
                both = jnp.where(low, upper, pltpu.roll(lower, HEAD, 1))
            else:
                both = jnp.where(low, pltpu.roll(upper, HEAD, 1), lower)
            xf[s2] = both.astype(BF16)

    def spread(t):
        sib_out(t, 0, xh).start()
        kv_out(t, 0, 1 - xh).start()
        for d in range(1, 8):
            @pl.when(z + d < 8)
            def _():
                for x2 in range(2):
                    kv_out(t, d, x2).start()

    def spread_done(t):
        sib_out(t, 0, xh).wait_send()
        kv_out(t, 0, 1 - xh).wait_send()
        for d in range(1, 8):
            @pl.when(z + d < 8)
            def _():
                for x2 in range(2):
                    kv_out(t, d, x2).wait_send()

    def relay(t, d):
        for x2 in range(2):
            kv_in(t, d, x2).wait_recv()
            sib_out(t, d, x2).start()

    def relay_own(t):
        kv_in(t, 0, 1 - xh).wait_recv()
        sib_out(t, 0, 1 - xh).start()

    def relay_done(t):
        sib_out(t, 0, 1 - xh).wait_send()
        for d in range(1, 8):
            @pl.when(d <= z)
            def _():
                for x2 in range(2):
                    sib_out(t, d, x2).wait_send()

    def place_queries(t, j, rows):
        @pl.when(me == j)
        def _():
            for p in range(2):
                qbuf[t][j, p] = rows[:, 128 * p:128 * p + 128]

        @pl.when(me != j)
        def _():
            for p in range(2):
                qst[t][j, p] = rows[:, 128 * p:128 * p + 128]
            q_out(t, j).start()

    def first_queries():
        normed = normalize(rows0[...], norm_gain[...])
        for j in range(KV_HEADS):
            rows = jnp.dot(normed, wq[:, 256 * j:256 * j + 256], preferred_element_type=F32)
            place_queries(0, j, (rows * QSCALE).astype(BF16))

    def queries(t):
        squares = jnp.zeros((ROWS, 1), F32)
        for n in range(4):
            @pl.when(s > 0)
            def _():
                h_out(t - 1, n).wait_recv()

            at = slice(512 * n, 512 * n + 512)
            wide = hid[t][n][...].astype(F32)
            squares += jnp.sum(wide * wide, axis=-1, keepdims=True)
            gained = (wide * norm_gain[:, at].astype(F32)).astype(BF16)
            for j in range(KV_HEADS):
                cols = slice(256 * j, 256 * j + 256)
                part = jnp.dot(gained, wq[at, cols], preferred_element_type=F32)
                if n == 0:
                    qacc[:, cols] = part
                elif n < 3:
                    qacc[:, cols] += part
                else:
                    factor = lax.rsqrt(squares / WIDTH + EPS) * QSCALE
                    place_queries(t, j, ((qacc[:, cols] + part) * factor).astype(BF16))

    key_row = lax.broadcasted_iota(jnp.int32, (128, 512), 0)
    key_lane = lax.broadcasted_iota(jnp.int32, (512, 128), 1)

    def prepare(t, d):
        for x2 in range(2):
            sib_in(t, d, x2).wait_recv()
        x = kv[t][d][...].reshape(512, 128).astype(F32)
        r = pltpu.roll(x, HEAD, 1)
        at = slice(512 * d, 512 * d + 512)
        ka[at, :] = jnp.where(key_lane < HEAD, x, 0.0).astype(BF16)
        kb[at, :] = jnp.where(key_lane < HEAD, 0.0, r).astype(BF16)
        vt[:, at] = jnp.where(key_row < HEAD, r.T, 1.0).astype(BF16)

    parts = [(h, slice(512 * half, 512 * half + 512)) for h in range(2) for half in range(2)]

    def keys_at(d):
        return pl.ds(pl.multiple_of(d * 512, 512), 512)

    def score(t, d, part, slot):
        h, cols = parts[part]
        layers = slice(2 * (part % 2), 2 * (part % 2) + 2)
        sc[slot] = lax.dot_general(
            (ka, kb)[h][keys_at(d), :], qbuf[t][layers].reshape(512, 128),
            (((1,), (1,)), ((), ())), preferred_element_type=F32,
        )

    def unit(t, d, after, masked):
        for part, (h, cols) in enumerate(parts):
            if part < 3:
                score(t, d, part + 1, (part + 1) % 2)
            elif after is not None:
                score(t, after, 0, 0)
            scores = sc[part % 2]
            if masked:
                kpos = lax.broadcasted_iota(jnp.int32, (512, 512), 0)
                qpos = lax.broadcasted_iota(jnp.int32, (512, 512), 1) % ROWS + xc * ROWS
                scores = jnp.where(kpos <= qpos, scores, NEG)
            scores = scores.reshape(64, 8, 512)
            top8 = jnp.max(scores, axis=0)
            for k in (4, 2, 1):
                top8 = jnp.maximum(top8, pltpu.roll(top8, k, 0))
            old = mx[h, :, cols]
            new = jnp.maximum(old, top8)
            decay = jnp.exp2(old - new)
            mx[h, :, cols] = new
            probs = jnp.exp2(scores - new[None]).astype(BF16).reshape(512, 512)
            grown = jnp.dot(vt[0:72, keys_at(d)], probs, preferred_element_type=F32)
            kept = (acc[h, :, cols].reshape(9, 8, 512) * decay[None]).reshape(72, 512)
            acc[h, :, cols] = kept + grown

    def wait_queries(t):
        for j in range(4):
            @pl.when(me != j)
            def _():
                q_in(t, j).wait_recv()

    def start_state():
        mx[...] = jnp.full(mx.shape, NEG, F32)
        acc[...] = jnp.zeros(acc.shape, F32)

    def first_units():
        start_state()
        relay_own(0)
        prepare(0, 0)

        @pl.when(z > 0)
        def _():
            relay(0, 1)

        wait_queries(0)
        score(0, 0, 0, 0)

        @pl.when(z > 0)
        def _():
            prepare(0, 1)

        unit(0, 0, jnp.minimum(z, 1), True)

        @pl.when(z > 1)
        def _():
            relay(0, 2)

        def step(d, carry):
            for near in range(1, 7):
                @pl.when((d == near) & (near < z))
                def _():
                    prepare(0, near + 1)

            unit(0, d, jnp.minimum(d + 1, z), False)
            for near in range(1, 6):
                @pl.when((d == near) & (near + 1 < z))
                def _():
                    relay(0, near + 2)

            return carry

        lax.fori_loop(1, z + 1, step, 0)

    def units(t):
        start_state()
        for d in range(7, 0, -1):
            @pl.when(d <= z)
            def _():
                prepare(t, d)

        wait_queries(t)
        prepare(t, 0)
        score(t, z, 0, 0)

        def step(i, carry):
            unit(t, z - i, z - i - 1, False)
            return carry

        lax.fori_loop(0, z, step, 0)
        unit(t, 0, None, True)

    def send_mixed(t):
        for i in range(4):
            for p in range(2):
                at = slice((2 * i + p) * 128, (2 * i + p) * 128 + 128)
                halves = [acc[h, 0:HEAD, at] / acc[h, HEAD:HEAD + 1, at] for h in range(2)]
                rows = jnp.concatenate(halves, axis=0).T.astype(BF16)

                @pl.when(me == i)
                def _():
                    mbuf[t][i, :, 128 * p:128 * p + 128] = rows

                @pl.when(me != i)
                def _():
                    mst[t][i, :, 128 * p:128 * p + 128] = rows

            @pl.when(me != i)
            def _():
                m_out(t, i).start()

    def finish(t):
        for j in range(4):
            @pl.when(me != j)
            def _():
                m_in(t, j).wait_recv()
        mixed = jnp.concatenate([mbuf[t][j] for j in range(4)], axis=1)
        for n in range(4):
            at = slice(512 * n, 512 * n + 512)
            grown = jnp.dot(mixed, wo[:, at], preferred_element_type=F32)
            before = rows0[:, at] if t == 0 else hid[t][n][...]
            out = (before.astype(F32) + grown).astype(BF16)
            if t + 1 == ITERS:
                layer_out[0, :, at] = out
            else:
                hout[t][n][...] = out

                @pl.when(s < 7)
                def _():
                    h_out(t, n).start()

    loads[0].wait()
    loads[1].wait()
    project(rows0[...], 0)
    kv[0][0][xc] = xs[0][me]
    spread(0)
    loads[2].wait()
    first_queries()

    @pl.when(s == 0)
    def _():
        for t in range(1, ITERS):
            for n in range(4):
                hid[t][n][...] = rows0[:, 512 * n:512 * n + 512]

    for t in range(ITERS):
        if t == 0:
            first_units()
        else:
            units(t)
        send_mixed(t)
        if t == 0:
            loads[3].wait()
        finish(t)
        if t + 1 < ITERS:
            @pl.when(top)
            def _():
                project(jnp.concatenate([hout[t][n][...] for n in range(4)], axis=1), t + 1)
                for s2 in range(7):
                    ks_out(t + 1, s2).start()
                kv[t + 1][0][xc] = xs[t + 1][3]

            @pl.when(s < 7)
            def _():
                ks_out(t + 1, 0).wait_recv()

            spread(t + 1)
            for d in range(7, 0, -1):
                @pl.when(d <= z)
                def _():
                    relay(t + 1, d)

            queries(t + 1)
            relay_own(t + 1)

    @pl.when(top)
    def _():
        project_last(layer_out[0])
        for s2 in range(7):
            ks_out(ITERS, s2).start()
        fin[c] = xf[7]

    @pl.when(s < 7)
    def _():
        ks_out(ITERS, 0).wait_recv()

    for d in range(1, 32):
        fin_out(d).start()

    def find(b, found):
        return jnp.where(block_slot[b] == c, b, found)

    block = lax.fori_loop(0, 32, find, jnp.int32(0))
    for d in range(1, 32):
        fin_in(d).wait_recv()
    rows = fin[block]
    decode[0, 0:HEAD, :] = rows[:, :HEAD]
    decode[0, HEAD:, :] = rows[:, HEAD:]

    for t in range(ITERS):
        spread_done(t)
        relay_done(t)
        for j in range(4):
            @pl.when(me != j)
            def _():
                q_out(t, j).wait_send()
                m_out(t, j).wait_send()
        if t + 1 < ITERS:
            @pl.when(s < 7)
            def _():
                for n in range(4):
                    h_out(t, n).wait_send()

        @pl.when(top)
        def _():
            for s2 in range(7):
                ks_out(t + 1, s2).wait_send()
    for d in range(1, 32):
        fin_out(d).wait_send()


def body(embeds, q_weight, out_weight, norm_gain, kv_weight, kv_gain, block_slot):
    vmem = pl.BlockSpec(memory_space=pltpu.VMEM)
    hbm = pl.BlockSpec(memory_space=pl.ANY)
    dma = pltpu.SemaphoreType.DMA
    return pl.pallas_call(
        kernel,
        out_shape=(
            jax.ShapeDtypeStruct((1, ROWS, WIDTH), BF16),
            jax.ShapeDtypeStruct((1, ROWS, HEAD), BF16),
        ),
        in_specs=[hbm, hbm, hbm, hbm, vmem, vmem, pl.BlockSpec(memory_space=pltpu.SMEM)],
        out_specs=(vmem, vmem),
        scratch_shapes=[
            pltpu.VMEM((WIDTH, 1024), BF16),
            pltpu.VMEM((1024, WIDTH), BF16),
            pltpu.VMEM((WIDTH, 512), BF16),
            (pltpu.VMEM((ROWS, WIDTH), BF16),) + (ITERS - 1) * (4 * (pltpu.VMEM((ROWS, 512), BF16),),),
            ITERS * (pltpu.VMEM((4, ROWS, 128), BF16),),
            pltpu.VMEM((8, HEAD, 128), BF16),
            ITERS * (8 * (pltpu.VMEM((4, ROWS, 128), BF16),),),
            ITERS * (pltpu.VMEM((4, 2, ROWS, 128), BF16),),
            ITERS * (pltpu.VMEM((4, 2, ROWS, 128), BF16),),
            ITERS * (pltpu.VMEM((4, ROWS, 256), BF16),),
            ITERS * (pltpu.VMEM((4, ROWS, 256), BF16),),
            (ITERS - 1) * (4 * (pltpu.VMEM((ROWS, 512), BF16),),),
            pltpu.VMEM((4096, 128), BF16),
            pltpu.VMEM((4096, 128), BF16),
            pltpu.VMEM((128, 4096), BF16),
            pltpu.VMEM((2, 8, 1024), F32),
            pltpu.VMEM((2, 72, 1024), F32),
            pltpu.VMEM((2, 512, 512), F32),
            pltpu.VMEM((ROWS, 1024), F32),
            pltpu.VMEM((32, HEAD, 128), BF16),
            dma((4,)),
            dma((ITERS, 16)), dma((ITERS, 16)), dma((ITERS, 16)), dma((ITERS, 16)),
            dma((ITERS, 4)), dma((ITERS, 4)), dma((ITERS, 4)), dma((ITERS, 4)),
            dma((ITERS, 4)), dma((ITERS, 4)), dma((ITERS, 8)), dma((ITERS,)),
            dma((32,)), dma((32,)),
        ],
        compiler_params=pltpu.CompilerParams(
            collective_id=0, has_side_effects=True, vmem_limit_bytes=56 << 20
        ),
        cost_estimate=pl.CostEstimate(
            flops=20 * 10**9, bytes_accessed=12 * 2**20, transcendentals=10**7
        ),
    )(embeds, q_weight, out_weight, kv_weight, norm_gain, kv_gain, block_slot)


def solution(mesh):
    return jax.shard_map(
        body,
        mesh=mesh,
        in_specs=(
            P("ctx", None),
            P("section", None, None),
            P("section", None, None),
            P("section", None),
            P(),
            P(),
            P(),
        ),
        out_specs=(P("section", "ctx", None), P("ctx", None, "section")),
        check_vma=False,
    )
```

```python
import jax
import jax.numpy as jnp
from jax import lax
from jax.experimental import pallas as pl
from jax.experimental.pallas import tpu as pltpu
from jax.sharding import PartitionSpec as P

BF16, F32 = jnp.bfloat16, jnp.float32
MESH = pl.DeviceIdType.MESH
WIDTH = 2048
ROWS = 128
HEADS = 16
KV_HEADS = 4
HEAD = 64
ITERS = 3
EPS = 1e-05
NEG = -1e30
QSCALE = HEAD**-0.5 * 1.4426950408889634


def normalize(rows, gain):
    wide = rows.astype(F32)
    factor = lax.rsqrt(jnp.mean(wide * wide, axis=-1, keepdims=True) + EPS)
    return (wide * factor * gain.astype(F32)).astype(BF16)


def kernel(
    embeds, q_weight, out_weight, kv_weight, norm_gain, kv_gain, block_slot,
    layer_out, decode,
    wq, wo, wkv, hid, xs, xf, kv, qst, qbuf, mst, mbuf, hout, ka, kb, vt, mx, acc, sc, qacc, fin,
    load_sem, kvd_s, kvd_r, x_s, x_r, sib_s, sib_r, q_s, q_r, m_s, m_r, h_s, h_r, ks_s, ks_r,
    fin_s, fin_r,
):
    s, c = lax.axis_index("section"), lax.axis_index("ctx")
    x_lo, y = s // 4, s % 4
    z, xh, core = c // 4, (c // 2) % 2, c % 2
    xc = c % 4
    top = s == 7
    me = x_lo * 2 + y % 2
    sib = z * 4 + xh * 2 + (1 - core)
    across = z * 4 + (1 - xh) * 2 + core

    rows0 = hid[0]
    loads = [
        pltpu.make_async_copy(src, dst, load_sem.at[i])
        for i, (src, dst) in enumerate(
            ((embeds, rows0), (kv_weight, wkv), (q_weight.at[0], wq), (out_weight.at[0], wo))
        )
    ]
    for copy in loads:
        copy.start()

    barrier = pltpu.get_barrier_semaphore()

    def greet(section, ctx):
        pl.semaphore_signal(barrier, inc=1, device_id=(section, ctx), device_id_type=MESH)

    for d in range(1, 8):
        greet((s + d) % 8, c)
    for d in range(1, 32):
        greet(s, (c + d) % 32)
    pl.semaphore_wait(barrier, 7 + 31)

    def send(src, dst, ssem, rsem, section, ctx):
        return pltpu.make_async_remote_copy(
            src_ref=src, dst_ref=dst, send_sem=ssem, recv_sem=rsem,
            device_id=(section, ctx), device_id_type=MESH,
        )

    def kv_out(t, d):
        return send(kv[t][0].at[xc], kv[t][d].at[xc], kvd_s.at[t, d], kvd_r.at[t, d], s, (z + d) * 4 + xc)

    def kv_in(t, d):
        return send(kv[t][d].at[xc], kv[t][d].at[xc], kvd_s.at[t, d], kvd_r.at[t, d], s, sib)

    def x_out(t, d):
        return send(kv[t][d].at[xc], kv[t][d].at[xc], x_s.at[t, d], x_r.at[t, d], s, across)

    def x_in(t, d):
        b = (1 - xh) * 2 + core
        return send(kv[t][d].at[b], kv[t][d].at[b], x_s.at[t, d], x_r.at[t, d], s, across)

    def sib_out(t, d, x2):
        b = x2 * 2 + core
        return send(kv[t][d].at[b], kv[t][d].at[b], sib_s.at[t, d * 2 + x2],
                    sib_r.at[t, d * 2 + x2], s, sib)

    def sib_in(t, d, x2):
        b = x2 * 2 + 1 - core
        return send(kv[t][d].at[b], kv[t][d].at[b], sib_s.at[t, d * 2 + x2],
                    sib_r.at[t, d * 2 + x2], s, sib)

    def member(m):
        return (m // 2) * 4 + (y // 2) * 2 + m % 2

    def q_out(t, j):
        return send(qst[t].at[j], qbuf[t].at[me], q_s.at[t, j], q_r.at[t, me], member(j), c)

    def q_in(t, j):
        return send(qst[t].at[j], qbuf[t].at[j], q_s.at[t, j], q_r.at[t, j], member(j), c)

    def m_out(t, i):
        return send(mst[t].at[i], mbuf[t].at[me], m_s.at[t, i], m_r.at[t, me], member(i), c)

    def m_in(t, j):
        return send(mst[t].at[j], mbuf[t].at[j], m_s.at[t, j], m_r.at[t, j], member(j), c)

    def h_out(t, n):
        return send(hout[t][n], hid[t + 1][n], h_s.at[t, n], h_r.at[t, n], (s + 1) % 8, c)

    def ks_out(t, s2):
        if t < ITERS:
            return send(xs[t].at[(s2 // 4) * 2 + s2 % 2], kv[t][0].at[xc], ks_s.at[t - 1, s2], ks_r.at[t - 1], s2, c)
        return send(xf.at[s2], fin.at[c], ks_s.at[t - 1, s2], ks_r.at[t - 1], s2, c)

    def fin_out(d):
        return send(fin.at[c], fin.at[c], fin_s.at[d], fin_r.at[d], s, (c + d) % 32)

    def fin_in(d):
        b = (c + 32 - d) % 32
        return send(fin.at[b], fin.at[b], fin_s.at[d], fin_r.at[d], s, b)

    lane = lax.broadcasted_iota(jnp.int32, (ROWS, 128), 1)

    def cache_rows(hidden):
        normed = normalize(hidden, kv_gain[...].reshape(1, WIDTH))
        return jnp.dot(normed, wkv[...], preferred_element_type=F32)

    def project(hidden, t):
        rows = cache_rows(hidden)
        for j in range(KV_HEADS):
            a, half = 128 * (j // 2), j % 2
            keys, values = rows[:, a:a + 128], rows[:, 256 + a:384 + a]
            if half == 0:
                both = jnp.where(lane < HEAD, keys, pltpu.roll(values, HEAD, 1))
            else:
                both = jnp.where(lane < HEAD, pltpu.roll(keys, HEAD, 1), values)
            xs[t][j] = both.astype(BF16)

    def project_last(hidden):
        rows = cache_rows(hidden)
        low = lane[:HEAD] < HEAD
        for s2 in range(8):
            a = 128 * (s2 // 2)
            upper, lower = rows[:HEAD, a:a + 128], rows[HEAD:, a:a + 128]
            if s2 % 2 == 0:
                both = jnp.where(low, upper, pltpu.roll(lower, HEAD, 1))
            else:
                both = jnp.where(low, pltpu.roll(upper, HEAD, 1), lower)
            xf[s2] = both.astype(BF16)

    def spread(t):
        sib_out(t, 0, xh).start()
        x_out(t, 0).start()
        for d in range(1, 8):
            @pl.when(z + d < 8)
            def _():
                kv_out(t, d).start()

    def relay(t, d):
        kv_in(t, d).wait_recv()
        sib_out(t, d, xh).start()
        x_out(t, d).start()

    def relay_across(t, d):
        x_in(t, d).wait_recv()
        sib_out(t, d, 1 - xh).start()

    def spread_done(t):
        for d in range(8):
            @pl.when(d <= z)
            def _():
                x_out(t, d).wait_send()
                for x2 in range(2):
                    sib_out(t, d, x2).wait_send()

            if d > 0:
                @pl.when(z + d < 8)
                def _():
                    kv_out(t, d).wait_send()

    def place_queries(t, j, rows):
        @pl.when(me == j)
        def _():
            for p in range(2):
                qbuf[t][j, p] = rows[:, 128 * p:128 * p + 128]

        @pl.when(me != j)
        def _():
            for p in range(2):
                qst[t][j, p] = rows[:, 128 * p:128 * p + 128]
            q_out(t, j).start()

    def first_queries():
        normed = normalize(rows0[...], norm_gain[...])
        for j in range(KV_HEADS):
            rows = jnp.dot(normed, wq[:, 256 * j:256 * j + 256], preferred_element_type=F32)
            place_queries(0, j, (rows * QSCALE).astype(BF16))

    def queries(t):
        squares = jnp.zeros((ROWS, 1), F32)
        for n in range(4):
            @pl.when(s > 0)
            def _():
                h_out(t - 1, n).wait_recv()

            at = slice(512 * n, 512 * n + 512)
            wide = hid[t][n][...].astype(F32)
            squares += jnp.sum(wide * wide, axis=-1, keepdims=True)
            gained = (wide * norm_gain[:, at].astype(F32)).astype(BF16)
            for j in range(KV_HEADS):
                cols = slice(256 * j, 256 * j + 256)
                part = jnp.dot(gained, wq[at, cols], preferred_element_type=F32)
                if n == 0:
                    qacc[:, cols] = part
                elif n < 3:
                    qacc[:, cols] += part
                else:
                    factor = lax.rsqrt(squares / WIDTH + EPS) * QSCALE
                    place_queries(t, j, ((qacc[:, cols] + part) * factor).astype(BF16))

    key_row = lax.broadcasted_iota(jnp.int32, (128, 512), 0)
    key_lane = lax.broadcasted_iota(jnp.int32, (512, 128), 1)

    def prepare(t, d):
        for x2 in range(2):
            sib_in(t, d, x2).wait_recv()
        x = kv[t][d][...].reshape(512, 128).astype(F32)
        r = pltpu.roll(x, HEAD, 1)
        at = slice(512 * d, 512 * d + 512)
        ka[at, :] = jnp.where(key_lane < HEAD, x, 0.0).astype(BF16)
        kb[at, :] = jnp.where(key_lane < HEAD, 0.0, r).astype(BF16)
        vt[:, at] = jnp.where(key_row < HEAD, r.T, 1.0).astype(BF16)

    parts = [(h, slice(512 * half, 512 * half + 512)) for h in range(2) for half in range(2)]

    def keys_at(d):
        return pl.ds(pl.multiple_of(d * 512, 512), 512)

    def score(t, d, part, slot):
        h, cols = parts[part]
        layers = slice(2 * (part % 2), 2 * (part % 2) + 2)
        sc[slot] = lax.dot_general(
            (ka, kb)[h][keys_at(d), :], qbuf[t][layers].reshape(512, 128),
            (((1,), (1,)), ((), ())), preferred_element_type=F32,
        )

    def unit(t, d, after, masked):
        for part, (h, cols) in enumerate(parts):
            if part < 3:
                score(t, d, part + 1, (part + 1) % 2)
            elif after is not None:
                score(t, after, 0, 0)
            scores = sc[part % 2]
            if masked:
                kpos = lax.broadcasted_iota(jnp.int32, (512, 512), 0)
                qpos = lax.broadcasted_iota(jnp.int32, (512, 512), 1) % ROWS + xc * ROWS
                scores = jnp.where(kpos <= qpos, scores, NEG)
            scores = scores.reshape(64, 8, 512)
            top8 = jnp.max(scores, axis=0)
            for k in (4, 2, 1):
                top8 = jnp.maximum(top8, pltpu.roll(top8, k, 0))
            old = mx[h, :, cols]
            new = jnp.maximum(old, top8)
            decay = jnp.exp2(old - new)
            mx[h, :, cols] = new
            probs = jnp.exp2(scores - new[None]).astype(BF16).reshape(512, 512)
            grown = jnp.dot(vt[0:72, keys_at(d)], probs, preferred_element_type=F32)
            kept = (acc[h, :, cols].reshape(9, 8, 512) * decay[None]).reshape(72, 512)
            acc[h, :, cols] = kept + grown

    def wait_queries(t):
        for j in range(4):
            @pl.when(me != j)
            def _():
                q_in(t, j).wait_recv()

    def start_state():
        mx[...] = jnp.full(mx.shape, NEG, F32)
        acc[...] = jnp.zeros(acc.shape, F32)

    def first_units():
        start_state()
        relay_across(0, 0)

        @pl.when(z > 0)
        def _():
            relay(0, 1)

        prepare(0, 0)
        wait_queries(0)
        score(0, 0, 0, 0)
        unit(0, 0, None, True)

        def pass_on(d):
            for near in range(0, 7):
                @pl.when((d == near) & (near < z))
                def _():
                    if near < 6:
                        @pl.when(near + 1 < z)
                        def _():
                            relay(0, near + 2)

                    relay_across(0, near + 1)

        pass_on(0)

        def step(d, carry):
            for near in range(1, 8):
                @pl.when(d == near)
                def _():
                    prepare(0, near)

            score(0, d, 0, 0)
            unit(0, d, None, False)
            pass_on(d)
            return carry

        lax.fori_loop(1, z + 1, step, 0)

    def units(t):
        start_state()
        for d in range(7, 0, -1):
            @pl.when(d <= z)
            def _():
                prepare(t, d)

        wait_queries(t)
        prepare(t, 0)
        score(t, z, 0, 0)

        def step(i, carry):
            unit(t, z - i, z - i - 1, False)
            return carry

        lax.fori_loop(0, z, step, 0)
        unit(t, 0, None, True)

    def send_mixed(t):
        for i in range(4):
            for p in range(2):
                at = slice((2 * i + p) * 128, (2 * i + p) * 128 + 128)
                halves = [acc[h, 0:HEAD, at] / acc[h, HEAD:HEAD + 1, at] for h in range(2)]
                rows = jnp.concatenate(halves, axis=0).T.astype(BF16)

                @pl.when(me == i)
                def _():
                    mbuf[t][i, :, 128 * p:128 * p + 128] = rows

                @pl.when(me != i)
                def _():
                    mst[t][i, :, 128 * p:128 * p + 128] = rows

            @pl.when(me != i)
            def _():
                m_out(t, i).start()

    def finish(t):
        for j in range(4):
            @pl.when(me != j)
            def _():
                m_in(t, j).wait_recv()
        mixed = jnp.concatenate([mbuf[t][j] for j in range(4)], axis=1)
        for n in range(4):
            at = slice(512 * n, 512 * n + 512)
            grown = jnp.dot(mixed, wo[:, at], preferred_element_type=F32)
            before = rows0[:, at] if t == 0 else hid[t][n][...]
            out = (before.astype(F32) + grown).astype(BF16)
            if t + 1 == ITERS:
                layer_out[0, :, at] = out
            else:
                hout[t][n][...] = out

                @pl.when(s < 7)
                def _():
                    h_out(t, n).start()

    loads[0].wait()
    loads[1].wait()
    project(rows0[...], 0)
    kv[0][0][xc] = xs[0][me]
    spread(0)
    loads[2].wait()
    first_queries()

    @pl.when(s == 0)
    def _():
        for t in range(1, ITERS):
            for n in range(4):
                hid[t][n][...] = rows0[:, 512 * n:512 * n + 512]

    for t in range(ITERS):
        if t == 0:
            first_units()
        else:
            units(t)
        send_mixed(t)
        if t == 0:
            loads[3].wait()
        finish(t)
        if t + 1 < ITERS:
            @pl.when(top)
            def _():
                project(jnp.concatenate([hout[t][n][...] for n in range(4)], axis=1), t + 1)
                for s2 in range(7):
                    ks_out(t + 1, s2).start()
                kv[t + 1][0][xc] = xs[t + 1][3]

            @pl.when(s < 7)
            def _():
                ks_out(t + 1, 0).wait_recv()

            spread(t + 1)
            for d in range(7, 0, -1):
                @pl.when(d <= z)
                def _():
                    relay(t + 1, d)

            queries(t + 1)
            for d in range(7, -1, -1):
                @pl.when(d <= z)
                def _():
                    relay_across(t + 1, d)

    @pl.when(top)
    def _():
        project_last(layer_out[0])
        for s2 in range(7):
            ks_out(ITERS, s2).start()
        fin[c] = xf[7]

    @pl.when(s < 7)
    def _():
        ks_out(ITERS, 0).wait_recv()

    for d in range(1, 32):
        fin_out(d).start()

    def find(b, found):
        return jnp.where(block_slot[b] == c, b, found)

    block = lax.fori_loop(0, 32, find, jnp.int32(0))
    for d in range(1, 32):
        fin_in(d).wait_recv()
    rows = fin[block]
    decode[0, 0:HEAD, :] = rows[:, :HEAD]
    decode[0, HEAD:, :] = rows[:, HEAD:]

    for t in range(ITERS):
        spread_done(t)
        for j in range(4):
            @pl.when(me != j)
            def _():
                q_out(t, j).wait_send()
                m_out(t, j).wait_send()
        if t + 1 < ITERS:
            @pl.when(s < 7)
            def _():
                for n in range(4):
                    h_out(t, n).wait_send()

        @pl.when(top)
        def _():
            for s2 in range(7):
                ks_out(t + 1, s2).wait_send()
    for d in range(1, 32):
        fin_out(d).wait_send()


def body(embeds, q_weight, out_weight, norm_gain, kv_weight, kv_gain, block_slot):
    vmem = pl.BlockSpec(memory_space=pltpu.VMEM)
    hbm = pl.BlockSpec(memory_space=pl.ANY)
    dma = pltpu.SemaphoreType.DMA
    return pl.pallas_call(
        kernel,
        out_shape=(
            jax.ShapeDtypeStruct((1, ROWS, WIDTH), BF16),
            jax.ShapeDtypeStruct((1, ROWS, HEAD), BF16),
        ),
        in_specs=[hbm, hbm, hbm, hbm, vmem, vmem, pl.BlockSpec(memory_space=pltpu.SMEM)],
        out_specs=(vmem, vmem),
        scratch_shapes=[
            pltpu.VMEM((WIDTH, 1024), BF16),
            pltpu.VMEM((1024, WIDTH), BF16),
            pltpu.VMEM((WIDTH, 512), BF16),
            (pltpu.VMEM((ROWS, WIDTH), BF16),) + (ITERS - 1) * (4 * (pltpu.VMEM((ROWS, 512), BF16),),),
            ITERS * (pltpu.VMEM((4, ROWS, 128), BF16),),
            pltpu.VMEM((8, HEAD, 128), BF16),
            ITERS * (8 * (pltpu.VMEM((4, ROWS, 128), BF16),),),
            ITERS * (pltpu.VMEM((4, 2, ROWS, 128), BF16),),
            ITERS * (pltpu.VMEM((4, 2, ROWS, 128), BF16),),
            ITERS * (pltpu.VMEM((4, ROWS, 256), BF16),),
            ITERS * (pltpu.VMEM((4, ROWS, 256), BF16),),
            (ITERS - 1) * (4 * (pltpu.VMEM((ROWS, 512), BF16),),),
            pltpu.VMEM((4096, 128), BF16),
            pltpu.VMEM((4096, 128), BF16),
            pltpu.VMEM((128, 4096), BF16),
            pltpu.VMEM((2, 8, 1024), F32),
            pltpu.VMEM((2, 72, 1024), F32),
            pltpu.VMEM((2, 512, 512), F32),
            pltpu.VMEM((ROWS, 1024), F32),
            pltpu.VMEM((32, HEAD, 128), BF16),
            dma((4,)),
            dma((ITERS, 8)), dma((ITERS, 8)), dma((ITERS, 8)), dma((ITERS, 8)), dma((ITERS, 16)), dma((ITERS, 16)),
            dma((ITERS, 4)), dma((ITERS, 4)), dma((ITERS, 4)), dma((ITERS, 4)),
            dma((ITERS, 4)), dma((ITERS, 4)), dma((ITERS, 8)), dma((ITERS,)),
            dma((32,)), dma((32,)),
        ],
        compiler_params=pltpu.CompilerParams(
            collective_id=0, has_side_effects=True, vmem_limit_bytes=56 << 20
        ),
        cost_estimate=pl.CostEstimate(
            flops=20 * 10**9, bytes_accessed=12 * 2**20, transcendentals=10**7
        ),
    )(embeds, q_weight, out_weight, kv_weight, norm_gain, kv_gain, block_slot)


def solution(mesh):
    return jax.shard_map(
        body,
        mesh=mesh,
        in_specs=(
            P("ctx", None),
            P("section", None, None),
            P("section", None, None),
            P("section", None),
            P(),
            P(),
            P(),
        ),
        out_specs=(P("section", "ctx", None), P("ctx", None, "section")),
        check_vma=False,
    )
```

```python
import jax
import jax.numpy as jnp
from jax import lax
from jax.experimental import pallas as pl
from jax.experimental.pallas import tpu as pltpu
from jax.sharding import PartitionSpec as P

BF16, F32 = jnp.bfloat16, jnp.float32
MESH = pl.DeviceIdType.MESH
WIDTH = 2048
ROWS = 128
HEADS = 16
KV_HEADS = 4
HEAD = 64
ITERS = 3
EPS = 1e-05
NEG = -1e30
QSCALE = HEAD**-0.5 * 1.4426950408889634


def normalize(rows, gain):
    wide = rows.astype(F32)
    factor = lax.rsqrt(jnp.mean(wide * wide, axis=-1, keepdims=True) + EPS)
    return (wide * factor * gain.astype(F32)).astype(BF16)


def kernel(
    embeds, q_weight, out_weight, kv_weight, norm_gain, kv_gain, block_slot,
    layer_out, decode,
    wq, wo, wkv, hid, xs, xf, kv, qst, qbuf, mst, mbuf, hout, ka, kb, vt, mx, acc, sc, qacc, fin,
    load_sem, kvd_s, kvd_r, sib_s, sib_r, q_s, q_r, m_s, m_r, h_s, h_r, ks_s, ks_r,
    fin_s, fin_r,
):
    s, c = lax.axis_index("section"), lax.axis_index("ctx")
    x_lo, y = s // 4, s % 4
    z, xh, core = c // 4, (c // 2) % 2, c % 2
    xc = c % 4
    top = s == 7
    me = x_lo * 2 + y % 2
    sib = z * 4 + xh * 2 + (1 - core)

    rows0 = hid[0]
    loads = [
        pltpu.make_async_copy(src, dst, load_sem.at[i])
        for i, (src, dst) in enumerate(
            ((embeds, rows0), (kv_weight, wkv), (q_weight.at[0], wq), (out_weight.at[0], wo))
        )
    ]
    for copy in loads:
        copy.start()

    barrier = pltpu.get_barrier_semaphore()

    def greet(section, ctx):
        pl.semaphore_signal(barrier, inc=1, device_id=(section, ctx), device_id_type=MESH)

    for d in range(1, 8):
        greet((s + d) % 8, c)
    for d in range(1, 32):
        greet(s, (c + d) % 32)
    pl.semaphore_wait(barrier, 7 + 31)

    def send(src, dst, ssem, rsem, section, ctx):
        return pltpu.make_async_remote_copy(
            src_ref=src, dst_ref=dst, send_sem=ssem, recv_sem=rsem,
            device_id=(section, ctx), device_id_type=MESH,
        )

    def kv_out(t, d, x2):
        return send(kv[t][0].at[xc], kv[t][d].at[xc], kvd_s.at[t, d * 2 + x2],
                    kvd_r.at[t, d * 2 + xh], s, (z + d) * 4 + x2 * 2 + core)

    def kv_in(t, d, x2):
        b = x2 * 2 + core
        return send(kv[t][d].at[b], kv[t][d].at[b], kvd_s.at[t, d * 2 + x2],
                    kvd_r.at[t, d * 2 + x2], s, sib)

    def sib_out(t, d, x2):
        b = x2 * 2 + core
        return send(kv[t][d].at[b], kv[t][d].at[b], sib_s.at[t, d * 2 + x2],
                    sib_r.at[t, d * 2 + x2], s, sib)

    def sib_in(t, d, x2):
        b = x2 * 2 + 1 - core
        return send(kv[t][d].at[b], kv[t][d].at[b], sib_s.at[t, d * 2 + x2],
                    sib_r.at[t, d * 2 + x2], s, sib)

    def member(m):
        return (m // 2) * 4 + (y // 2) * 2 + m % 2

    def q_out(t, j):
        return send(qst[t].at[j], qbuf[t].at[me], q_s.at[t, j], q_r.at[t, me], member(j), c)

    def q_in(t, j):
        return send(qst[t].at[j], qbuf[t].at[j], q_s.at[t, j], q_r.at[t, j], member(j), c)

    def m_out(t, i):
        return send(mst[t].at[i], mbuf[t].at[me], m_s.at[t, i], m_r.at[t, me], member(i), c)

    def m_in(t, j):
        return send(mst[t].at[j], mbuf[t].at[j], m_s.at[t, j], m_r.at[t, j], member(j), c)

    def h_out(t, n):
        return send(hout[t][n], hid[t + 1][n], h_s.at[t, n], h_r.at[t, n], (s + 1) % 8, c)

    def ks_out(t, s2):
        if t < ITERS:
            return send(xs[t].at[(s2 // 4) * 2 + s2 % 2], kv[t][0].at[xc], ks_s.at[t - 1, s2], ks_r.at[t - 1], s2, c)
        return send(xf.at[s2], fin.at[c], ks_s.at[t - 1, s2], ks_r.at[t - 1], s2, c)

    def fin_out(d):
        return send(fin.at[c], fin.at[c], fin_s.at[d], fin_r.at[d], s, (c + d) % 32)

    def fin_in(d):
        b = (c + 32 - d) % 32
        return send(fin.at[b], fin.at[b], fin_s.at[d], fin_r.at[d], s, b)

    lane = lax.broadcasted_iota(jnp.int32, (ROWS, 128), 1)

    def cache_rows(hidden):
        normed = normalize(hidden, kv_gain[...].reshape(1, WIDTH))
        return jnp.dot(normed, wkv[...], preferred_element_type=F32)

    def project(hidden, t):
        rows = cache_rows(hidden)
        for j in range(KV_HEADS):
            a, half = 128 * (j // 2), j % 2
            keys, values = rows[:, a:a + 128], rows[:, 256 + a:384 + a]
            if half == 0:
                both = jnp.where(lane < HEAD, keys, pltpu.roll(values, HEAD, 1))
            else:
                both = jnp.where(lane < HEAD, pltpu.roll(keys, HEAD, 1), values)
            xs[t][j] = both.astype(BF16)

    def project_last(hidden):
        rows = cache_rows(hidden)
        low = lane[:HEAD] < HEAD
        for s2 in range(8):
            a = 128 * (s2 // 2)
            upper, lower = rows[:HEAD, a:a + 128], rows[HEAD:, a:a + 128]
            if s2 % 2 == 0:
                both = jnp.where(low, upper, pltpu.roll(lower, HEAD, 1))
            else:
                both = jnp.where(low, pltpu.roll(upper, HEAD, 1), lower)
            xf[s2] = both.astype(BF16)

    def spread(t):
        sib_out(t, 0, xh).start()
        kv_out(t, 0, 1 - xh).start()
        for d in range(1, 8):
            @pl.when(z + d < 8)
            def _():
                for x2 in range(2):
                    kv_out(t, d, x2).start()

    def spread_done(t):
        sib_out(t, 0, xh).wait_send()
        kv_out(t, 0, 1 - xh).wait_send()
        for d in range(1, 8):
            @pl.when(z + d < 8)
            def _():
                for x2 in range(2):
                    kv_out(t, d, x2).wait_send()

    def relay(t, d):
        for x2 in range(2):
            kv_in(t, d, x2).wait_recv()
            sib_out(t, d, x2).start()

    def relay_own(t):
        kv_in(t, 0, 1 - xh).wait_recv()
        sib_out(t, 0, 1 - xh).start()

    def relay_done(t):
        sib_out(t, 0, 1 - xh).wait_send()
        for d in range(1, 8):
            @pl.when(d <= z)
            def _():
                for x2 in range(2):
                    sib_out(t, d, x2).wait_send()

    def place_queries(t, j, rows):
        @pl.when(me == j)
        def _():
            for p in range(2):
                qbuf[t][j, p] = rows[:, 128 * p:128 * p + 128]

        @pl.when(me != j)
        def _():
            for p in range(2):
                qst[t][j, p] = rows[:, 128 * p:128 * p + 128]
            q_out(t, j).start()

    def first_queries():
        normed = normalize(rows0[...], norm_gain[...])
        for j in range(KV_HEADS):
            rows = jnp.dot(normed, wq[:, 256 * j:256 * j + 256], preferred_element_type=F32)
            place_queries(0, j, (rows * QSCALE).astype(BF16))

    def queries(t):
        squares = jnp.zeros((ROWS, 1), F32)
        for n in range(4):
            @pl.when(s > 0)
            def _():
                h_out(t - 1, n).wait_recv()

            at = slice(512 * n, 512 * n + 512)
            wide = hid[t][n][...].astype(F32)
            squares += jnp.sum(wide * wide, axis=-1, keepdims=True)
            gained = (wide * norm_gain[:, at].astype(F32)).astype(BF16)
            for j in range(KV_HEADS):
                cols = slice(256 * j, 256 * j + 256)
                part = jnp.dot(gained, wq[at, cols], preferred_element_type=F32)
                if n == 0:
                    qacc[:, cols] = part
                elif n < 3:
                    qacc[:, cols] += part
                else:
                    factor = lax.rsqrt(squares / WIDTH + EPS) * QSCALE
                    place_queries(t, j, ((qacc[:, cols] + part) * factor).astype(BF16))

    key_row = lax.broadcasted_iota(jnp.int32, (128, 512), 0)
    key_lane = lax.broadcasted_iota(jnp.int32, (512, 128), 1)

    def prepare(t, d):
        for x2 in range(2):
            sib_in(t, d, x2).wait_recv()
        x = kv[t][d][...].reshape(512, 128).astype(F32)
        r = pltpu.roll(x, HEAD, 1)
        at = slice(512 * d, 512 * d + 512)
        ka[at, :] = jnp.where(key_lane < HEAD, x, 0.0).astype(BF16)
        kb[at, :] = jnp.where(key_lane < HEAD, 0.0, r).astype(BF16)
        vt[:, at] = jnp.where(key_row < HEAD, r.T, 1.0).astype(BF16)

    parts = [(h, slice(512 * half, 512 * half + 512)) for h in range(2) for half in range(2)]

    def keys_at(d):
        return pl.ds(pl.multiple_of(d * 512, 512), 512)

    def score(t, d, part, slot):
        h, cols = parts[part]
        layers = slice(2 * (part % 2), 2 * (part % 2) + 2)
        sc[slot] = lax.dot_general(
            (ka, kb)[h][keys_at(d), :], qbuf[t][layers].reshape(512, 128),
            (((1,), (1,)), ((), ())), preferred_element_type=F32,
        )

    def unit(t, d, after, masked):
        for part, (h, cols) in enumerate(parts):
            if part < 3:
                score(t, d, part + 1, (part + 1) % 2)
            elif after is not None:
                score(t, after, 0, 0)
            scores = sc[part % 2]
            if masked:
                kpos = lax.broadcasted_iota(jnp.int32, (512, 512), 0)
                qpos = lax.broadcasted_iota(jnp.int32, (512, 512), 1) % ROWS + xc * ROWS
                scores = jnp.where(kpos <= qpos, scores, NEG)
            scores = scores.reshape(64, 8, 512)
            top8 = jnp.max(scores, axis=0)
            for k in (4, 2, 1):
                top8 = jnp.maximum(top8, pltpu.roll(top8, k, 0))
            old = mx[h, :, cols]
            new = jnp.maximum(old, top8)
            decay = jnp.exp2(old - new)
            mx[h, :, cols] = new
            probs = jnp.exp2(scores - new[None]).astype(BF16).reshape(512, 512)
            grown = jnp.dot(vt[0:72, keys_at(d)], probs, preferred_element_type=F32)
            kept = (acc[h, :, cols].reshape(9, 8, 512) * decay[None]).reshape(72, 512)
            acc[h, :, cols] = kept + grown

    def wait_queries(t):
        for j in range(4):
            @pl.when(me != j)
            def _():
                q_in(t, j).wait_recv()

    def start_state():
        mx[...] = jnp.full(mx.shape, NEG, F32)
        acc[...] = jnp.zeros(acc.shape, F32)

    def first_units():
        start_state()
        relay_own(0)
        prepare(0, 0)

        @pl.when(z > 0)
        def _():
            relay(0, 1)

        wait_queries(0)
        score(0, 0, 0, 0)
        unit(0, 0, None, True)

        def step(d, carry):
            for near in range(1, 8):
                @pl.when(d == near)
                def _():
                    if near < 7:
                        @pl.when(near < z)
                        def _():
                            relay(0, near + 1)

                    prepare(0, near)

            score(0, d, 0, 0)
            unit(0, d, None, False)
            return carry

        lax.fori_loop(1, z + 1, step, 0)

    def units(t):
        start_state()
        for d in range(7, 0, -1):
            @pl.when(d <= z)
            def _():
                prepare(t, d)

        wait_queries(t)
        prepare(t, 0)
        score(t, z, 0, 0)

        def step(i, carry):
            unit(t, z - i, z - i - 1, False)
            return carry

        lax.fori_loop(0, z, step, 0)
        unit(t, 0, None, True)

    def send_mixed(t):
        for i in range(4):
            for p in range(2):
                at = slice((2 * i + p) * 128, (2 * i + p) * 128 + 128)
                halves = [acc[h, 0:HEAD, at] / acc[h, HEAD:HEAD + 1, at] for h in range(2)]
                rows = jnp.concatenate(halves, axis=0).T.astype(BF16)

                @pl.when(me == i)
                def _():
                    mbuf[t][i, :, 128 * p:128 * p + 128] = rows

                @pl.when(me != i)
                def _():
                    mst[t][i, :, 128 * p:128 * p + 128] = rows

            @pl.when(me != i)
            def _():
                m_out(t, i).start()

    def finish(t):
        for j in range(4):
            @pl.when(me != j)
            def _():
                m_in(t, j).wait_recv()
        mixed = jnp.concatenate([mbuf[t][j] for j in range(4)], axis=1)
        for n in range(4):
            at = slice(512 * n, 512 * n + 512)
            grown = jnp.dot(mixed, wo[:, at], preferred_element_type=F32)
            before = rows0[:, at] if t == 0 else hid[t][n][...]
            out = (before.astype(F32) + grown).astype(BF16)
            if t + 1 == ITERS:
                layer_out[0, :, at] = out
            else:
                hout[t][n][...] = out

                @pl.when(s < 7)
                def _():
                    h_out(t, n).start()

    loads[0].wait()
    loads[1].wait()
    project(rows0[...], 0)
    kv[0][0][xc] = xs[0][me]
    spread(0)
    loads[2].wait()
    first_queries()

    @pl.when(s == 0)
    def _():
        for t in range(1, ITERS):
            for n in range(4):
                hid[t][n][...] = rows0[:, 512 * n:512 * n + 512]

    for t in range(ITERS):
        if t == 0:
            first_units()
        else:
            units(t)
        send_mixed(t)
        if t == 0:
            loads[3].wait()
        finish(t)
        if t + 1 < ITERS:
            @pl.when(top)
            def _():
                project(jnp.concatenate([hout[t][n][...] for n in range(4)], axis=1), t + 1)
                for s2 in range(7):
                    ks_out(t + 1, s2).start()
                kv[t + 1][0][xc] = xs[t + 1][3]

            @pl.when(s < 7)
            def _():
                ks_out(t + 1, 0).wait_recv()

            spread(t + 1)
            for d in range(7, 0, -1):
                @pl.when(d <= z)
                def _():
                    relay(t + 1, d)

            queries(t + 1)
            relay_own(t + 1)

    @pl.when(top)
    def _():
        project_last(layer_out[0])
        for s2 in range(7):
            ks_out(ITERS, s2).start()
        fin[c] = xf[7]

    @pl.when(s < 7)
    def _():
        ks_out(ITERS, 0).wait_recv()

    for d in range(1, 32):
        fin_out(d).start()

    def find(b, found):
        return jnp.where(block_slot[b] == c, b, found)

    block = lax.fori_loop(0, 32, find, jnp.int32(0))
    for d in range(1, 32):
        fin_in(d).wait_recv()
    rows = fin[block]
    decode[0, 0:HEAD, :] = rows[:, :HEAD]
    decode[0, HEAD:, :] = rows[:, HEAD:]

    for t in range(ITERS):
        spread_done(t)
        relay_done(t)
        for j in range(4):
            @pl.when(me != j)
            def _():
                q_out(t, j).wait_send()
                m_out(t, j).wait_send()
        if t + 1 < ITERS:
            @pl.when(s < 7)
            def _():
                for n in range(4):
                    h_out(t, n).wait_send()

        @pl.when(top)
        def _():
            for s2 in range(7):
                ks_out(t + 1, s2).wait_send()
    for d in range(1, 32):
        fin_out(d).wait_send()


def body(embeds, q_weight, out_weight, norm_gain, kv_weight, kv_gain, block_slot):
    vmem = pl.BlockSpec(memory_space=pltpu.VMEM)
    hbm = pl.BlockSpec(memory_space=pl.ANY)
    dma = pltpu.SemaphoreType.DMA
    return pl.pallas_call(
        kernel,
        out_shape=(
            jax.ShapeDtypeStruct((1, ROWS, WIDTH), BF16),
            jax.ShapeDtypeStruct((1, ROWS, HEAD), BF16),
        ),
        in_specs=[hbm, hbm, hbm, hbm, vmem, vmem, pl.BlockSpec(memory_space=pltpu.SMEM)],
        out_specs=(vmem, vmem),
        scratch_shapes=[
            pltpu.VMEM((WIDTH, 1024), BF16),
            pltpu.VMEM((1024, WIDTH), BF16),
            pltpu.VMEM((WIDTH, 512), BF16),
            (pltpu.VMEM((ROWS, WIDTH), BF16),) + (ITERS - 1) * (4 * (pltpu.VMEM((ROWS, 512), BF16),),),
            ITERS * (pltpu.VMEM((4, ROWS, 128), BF16),),
            pltpu.VMEM((8, HEAD, 128), BF16),
            ITERS * (8 * (pltpu.VMEM((4, ROWS, 128), BF16),),),
            ITERS * (pltpu.VMEM((4, 2, ROWS, 128), BF16),),
            ITERS * (pltpu.VMEM((4, 2, ROWS, 128), BF16),),
            ITERS * (pltpu.VMEM((4, ROWS, 256), BF16),),
            ITERS * (pltpu.VMEM((4, ROWS, 256), BF16),),
            (ITERS - 1) * (4 * (pltpu.VMEM((ROWS, 512), BF16),),),
            pltpu.VMEM((4096, 128), BF16),
            pltpu.VMEM((4096, 128), BF16),
            pltpu.VMEM((128, 4096), BF16),
            pltpu.VMEM((2, 8, 1024), F32),
            pltpu.VMEM((2, 72, 1024), F32),
            pltpu.VMEM((2, 512, 512), F32),
            pltpu.VMEM((ROWS, 1024), F32),
            pltpu.VMEM((32, HEAD, 128), BF16),
            dma((4,)),
            dma((ITERS, 16)), dma((ITERS, 16)), dma((ITERS, 16)), dma((ITERS, 16)),
            dma((ITERS, 4)), dma((ITERS, 4)), dma((ITERS, 4)), dma((ITERS, 4)),
            dma((ITERS, 4)), dma((ITERS, 4)), dma((ITERS, 8)), dma((ITERS,)),
            dma((32,)), dma((32,)),
        ],
        compiler_params=pltpu.CompilerParams(
            collective_id=0, has_side_effects=True, vmem_limit_bytes=56 << 20
        ),
        cost_estimate=pl.CostEstimate(
            flops=20 * 10**9, bytes_accessed=12 * 2**20, transcendentals=10**7
        ),
    )(embeds, q_weight, out_weight, kv_weight, norm_gain, kv_gain, block_slot)


def solution(mesh):
    return jax.shard_map(
        body,
        mesh=mesh,
        in_specs=(
            P("ctx", None),
            P("section", None, None),
            P("section", None, None),
            P("section", None),
            P(),
            P(),
            P(),
        ),
        out_specs=(P("section", "ctx", None), P("ctx", None, "section")),
        check_vma=False,
    )
```
